512 devices in a mesh: seq: 64 (over z, y), head: 8 (over x, core).
Axes of the slice: x: 4, y: 4, z: 16, core: 2. Of those that a mesh axis runs over, the one named last changes fastest.
Arguments:
- store_hidden: bfloat16 [16384, 8192], P('seq', 'head'), may hold values from -320 to 320
- owner_map: int32 [16384, 1], P('seq'), may hold values from 0 to 63, as said below
- new_hidden: bfloat16 [8192, 8192], P('seq', 'head'), may hold values from -320 to 320
- new_lengths: int32 [64], P('seq'), may hold values from 1 to 128, as said below
- queries: bfloat16 [8192, 8192], P('seq', 'head'), may hold values from -240 to 240
- key_weight: bfloat16 [8192, 1024], P('head', 'seq'), may hold values from -0.013671875 to 0.013671875
- value_weight: bfloat16 [8192, 1024], P('head', 'seq'), may hold values from -0.013671875 to 0.013671875
Outputs:
- attended: bfloat16 [8192, 8192], P('seq', 'head')
- key_cache: bfloat16 [64, 640, 1024], P('seq', None, 'head')
- value_cache: bfloat16 [64, 640, 1024], P('seq', None, 'head')
The draws below stay inside these ranges and needn't reach their ends.
Inputs may be any that keep to these rules, and one draw needn't show every extreme that they name: `owner_map`: within the 256 rows of one store shard no session owns more than 8 rows; in every draw one session owns exactly 8 rows of every shard, so its history is 512 rows; every session owns at least one row. `new_lengths`: some session's new turn has exactly 128 tokens.
All inputs are finite; a program needn't handle non-finite values.
Results may differ from the reference program's by a relative error of at most 0.033.
Values may be sent and summed in bfloat16 or wider, within the bound.
A program may use at most 64 MiB of HBM per device.

```python
import jax
import jax.numpy as jnp
from jax import lax

D = 8192
QH = 64
KVH = 8
HD = 128
ROWS_DEV = 256
NEW = 128
SESS = 64
CAP = 8
HIST_CAP = 512
CACHE = 640
TOTAL_ROWS = 16384
NEW_ROWS = 8192
N_HEAD = 8


def rough_rows(key, count, rise, spread):
    noise_key, rough_key, row_key = jax.random.split(key, 3)
    column = jnp.arange(D, dtype=jnp.float32) / D
    trend = 0.6 * jnp.power(rise, column) * jax.random.uniform(rough_key, (D,), jnp.float32, 0.7, 1.4)
    values = jnp.clip(jax.random.normal(noise_key, (count, D), jnp.float32), -4.0, 4.0)
    row_scale = jnp.power(spread, jax.random.uniform(row_key, (count, 1), jnp.float32))
    return (values * trend[None, :] * row_scale).astype(jnp.bfloat16)


def draw_store_hidden(key, part):
    key = jax.random.fold_in(key, 3)
    return rough_rows(key, TOTAL_ROWS, 3.0, 1.0)


def draw_new_hidden(key, part):
    key = jax.random.fold_in(key, 5)
    return rough_rows(key, NEW_ROWS, 3.0, 1.0)


def shard_owners(shard_key, shard, full_session):
    score_key, order_key = jax.random.split(shard_key)
    slot_index = jnp.arange(SESS * CAP, dtype=jnp.int32)
    slot_session = slot_index // CAP
    scores = jax.random.randint(score_key, (SESS * CAP,), 0, 2 ** 18, dtype=jnp.int32) * (SESS * CAP) + slot_index
    scores = jnp.where(slot_session == full_session, 2 ** 30, scores)
    scores = jnp.where((slot_index == shard * CAP) & (shard != full_session), -1, scores)
    ordering = jnp.argsort(scores, stable=True)
    chosen = slot_session[ordering[:ROWS_DEV - CAP]]
    owners = jnp.concatenate([jnp.full((CAP,), full_session, jnp.int32), chosen])
    return jax.random.permutation(order_key, owners)


def draw_owner_map(key, part):
    key = jax.random.fold_in(key, 11)
    full_key, shard_key = jax.random.split(key)
    full_session = jax.random.randint(full_key, (), 0, SESS, dtype=jnp.int32)
    shard_keys = jax.random.split(shard_key, SESS)
    shards = jnp.arange(SESS, dtype=jnp.int32)
    owners = jax.vmap(shard_owners, in_axes=(0, 0, None))(shard_keys, shards, full_session)
    return owners.reshape(TOTAL_ROWS, 1)


def draw_new_lengths(key, part):
    key = jax.random.fold_in(key, 17)
    length_key, pick_key = jax.random.split(key)
    lengths = jax.random.randint(length_key, (SESS,), 1, NEW + 1, dtype=jnp.int32)
    picked = jax.random.randint(pick_key, (), 0, SESS, dtype=jnp.int32)
    return jnp.where(jnp.arange(SESS, dtype=jnp.int32) == picked, NEW, lengths)


def draw_queries(key, part):
    key = jax.random.fold_in(key, 31)
    noise_key, scale_key = jax.random.split(key)
    values = jnp.clip(jax.random.normal(noise_key, (NEW_ROWS, QH, HD), jnp.float32), -4.0, 4.0)
    head_scale = jnp.exp(jax.random.uniform(scale_key, (NEW_ROWS, QH, 1), jnp.float32, -0.69, 0.69))
    return (values * head_scale).reshape(NEW_ROWS, QH * HD).astype(jnp.bfloat16)


def level_of(rng, dims, pieces, least, top_value):
    level, own = 1.0, jax.random.fold_in(rng, 6)
    for position, parts in pieces:
        draws = jnp.exp(jax.random.uniform(jax.random.fold_in(own, position), (parts,), jnp.float32, least / len(pieces), top_value / len(pieces)))
        level = level * jnp.repeat(draws, dims[position] // parts).reshape([-1 if axis == position else 1 for axis in range(len(dims))])
    return level


def scatter_about(key, dims, scale, most, pieces=(), kind=jnp.bfloat16):
    level = level_of(key, dims, pieces, -0.22, 0.18) if pieces else 1.0
    values = jax.random.normal(key, dims, jnp.float32) * scale * level
    return jnp.minimum(jnp.maximum(values, -most), most).astype(kind)


def setup_inputs(seed: int = 0) -> dict:
    arg_keys = jax.random.split(jax.random.key(seed), 8)
    return {
        "store_hidden": draw_store_hidden(jax.random.fold_in(arg_keys[7], 71), 0),
        "owner_map": draw_owner_map(jax.random.fold_in(arg_keys[7], 71), 0),
        "new_hidden": draw_new_hidden(jax.random.fold_in(arg_keys[7], 71), 0),
        "new_lengths": draw_new_lengths(jax.random.fold_in(arg_keys[7], 71), 0),
        "queries": draw_queries(jax.random.fold_in(arg_keys[7], 71), 0),
        "key_weight": scatter_about(arg_keys[5], (D, KVH * HD), (25 * D) ** -0.5, 0.013671875, ((0, 8), (1, 64))),
        "value_weight": scatter_about(arg_keys[6], (D, KVH * HD), (25 * D) ** -0.5, 0.013671875, ((0, 8), (1, 64))),
    }


rope_base = 500000.0

def frequencies():
    half_index = jnp.arange(HD // 2, dtype=jnp.float32)
    inverse = 1.0 / jnp.power(rope_base, 2.0 * half_index / HD)
    wavelength = 2.0 * jnp.pi / inverse
    smooth = (8192.0 / wavelength - 1.0) / 3.0
    mixed = (1.0 - smooth) * inverse / 8.0 + smooth * inverse
    return jnp.where(wavelength < 2048.0, inverse, jnp.where(wavelength > 8192.0, inverse / 8.0, mixed))

def rotate(values, angles):
    cosine = jnp.cos(angles)
    sine = jnp.sin(angles)
    first = values[..., :HD // 2]
    second = values[..., HD // 2:]
    return jnp.concatenate([first * cosine - second * sine, second * cosine + first * sine], axis=-1)

def project(hidden_rows, weights):
    width = D // N_HEAD
    totals = jnp.zeros((hidden_rows.shape[0], weights.shape[1]), jnp.float32)
    for member in range(N_HEAD):
        partial_rows = jnp.dot(hidden_rows[:, member * width:(member + 1) * width], weights[member * width:(member + 1) * width], preferred_element_type=jnp.float32)
        rounded = lax.optimization_barrier(partial_rows.astype(jnp.bfloat16))
        totals = totals + rounded.astype(jnp.float32)
    squares = lax.optimization_barrier(jnp.sum(jnp.square(hidden_rows.astype(jnp.float32)), axis=1))
    scales = lax.rsqrt(squares / D + 1e-05)
    return totals * scales[:, None]

def reference(store_hidden, owner_map, new_hidden, new_lengths, queries, key_weight, value_weight):
    frequency = frequencies()
    weights = jnp.concatenate([key_weight, value_weight], axis=1)
    owners = owner_map[:, 0].astype(jnp.int32)
    owner_hits = (owners[:, None] == jnp.arange(SESS, dtype=jnp.int32)[None, :]).astype(jnp.int32)
    row_ranks = lax.optimization_barrier(jnp.sum((jnp.cumsum(owner_hits, axis=0).astype(jnp.int32) - owner_hits) * owner_hits, axis=1)).astype(jnp.int32)
    lengths = lax.optimization_barrier(jnp.sum(owner_hits, axis=0)).astype(jnp.int32)
    stored = project(store_hidden, weights)
    stored_keys = stored[:, :KVH * HD].reshape(TOTAL_ROWS, KVH, HD)
    stored_angles = row_ranks.astype(jnp.float32)[:, None, None] * frequency[None, None, :]
    history_keys = rotate(stored_keys, stored_angles).astype(jnp.bfloat16).reshape(TOTAL_ROWS, KVH * HD)
    history_values = stored[:, KVH * HD:].astype(jnp.bfloat16)
    key_history = jnp.zeros((SESS, HIST_CAP, KVH * HD), jnp.bfloat16).at[owners, row_ranks].set(history_keys)
    value_history = jnp.zeros((SESS, HIST_CAP, KVH * HD), jnp.bfloat16).at[owners, row_ranks].set(history_values)
    fresh_rows = project(new_hidden, weights).reshape(SESS, NEW, 2 * KVH * HD)
    turn_index = jnp.arange(NEW, dtype=jnp.int32)
    fresh_positions = (lengths[:, None] + turn_index[None, :]).astype(jnp.float32)
    live_rows = turn_index[None, :] < new_lengths[:, None]
    fresh_angles = fresh_positions[:, :, None, None] * frequency[None, None, None, :]
    fresh_keys = rotate(fresh_rows[..., :KVH * HD].reshape(SESS, NEW, KVH, HD), fresh_angles).reshape(SESS, NEW, KVH * HD)
    fresh_keys = jnp.where(live_rows[:, :, None], fresh_keys, 0.0).astype(jnp.bfloat16)
    fresh_values = jnp.where(live_rows[:, :, None], fresh_rows[..., KVH * HD:], 0.0).astype(jnp.bfloat16)
    key_cache = jnp.concatenate([key_history, fresh_keys], axis=1)
    value_cache = jnp.concatenate([value_history, fresh_values], axis=1)
    query_heads = queries.reshape(SESS, NEW, QH, HD).astype(jnp.float32)
    rotated_queries = rotate(query_heads, fresh_angles).astype(jnp.bfloat16)
    group = QH // KVH

    def attend(session_item):
        query_rows, key_rows, value_rows, length, turn_length = session_item
        query_four = query_rows.reshape(NEW, KVH, group, HD).astype(jnp.float32)
        key_three = key_rows.reshape(CACHE, KVH, HD).astype(jnp.float32)
        value_three = value_rows.reshape(CACHE, KVH, HD).astype(jnp.float32)
        scores = jnp.einsum('jkgh,ckh->kgjc', query_four, key_three) / jnp.sqrt(jnp.float32(HD))
        column = jnp.arange(CACHE, dtype=jnp.int32)
        allowed = (column[None, :] < length) | (column[None, :] >= HIST_CAP) & (column[None, :] - HIST_CAP <= turn_index[:, None])
        scores = jnp.where(allowed[None, None], scores, -jnp.inf)
        highest = lax.optimization_barrier(jnp.max(scores, axis=-1, keepdims=True))
        exponent = jnp.exp(scores - highest)
        attention_weights = (exponent / lax.optimization_barrier(jnp.sum(exponent, axis=-1, keepdims=True))).astype(jnp.bfloat16)
        result = jnp.einsum('kgjc,ckh->jkgh', attention_weights.astype(jnp.float32), value_three)
        result = jnp.where((turn_index < turn_length)[:, None, None, None], result, 0.0)
        return result.astype(jnp.bfloat16).reshape(NEW, QH * HD)
    attended = lax.map(attend, (rotated_queries, key_cache, value_cache, lengths, new_lengths))
    return (attended.reshape(NEW_ROWS, QH * HD), key_cache, value_cache)
```

```python
import functools
import math

import jax
import jax.numpy as jnp
import numpy as np
from jax import lax
from jax.experimental import pallas as pl
from jax.experimental.pallas import tpu as pltpu
from jax.sharding import PartitionSpec as P

D = 8192
QH = 64
KVH = 8
HD = 128
NZ = 16
NY = 4
NX = 4
STORED = 256
TURN = 128
ROWS = STORED + TURN
CAP = 8
SESS = NZ * NY
HIST = SESS * CAP
CACHE = HIST + TURN
FEAT = D // (2 * NX)
CHIP_FEAT = 2 * FEAT
SPLIT = 1280
EMPTY = float(2.0**100)
EMPTY_TEST = float(2.0**50)
MESH = pl.DeviceIdType.MESH
rope_base = 500000.0


def rotation_tables():
    half_index = np.arange(HD // 2, dtype=np.float64)
    inverse = 1.0 / np.power(rope_base, 2.0 * half_index / HD)
    wavelength = 2.0 * np.pi / inverse
    smooth = (8192.0 / wavelength - 1.0) / 3.0
    mixed = (1.0 - smooth) * inverse / 8.0 + smooth * inverse
    frequency = np.where(
        wavelength < 2048.0, inverse, np.where(wavelength > 8192.0, inverse / 8.0, mixed)
    )
    angles = np.arange(CACHE, dtype=np.float64)[:, None] * frequency[None, :]
    cosine, sine = np.cos(angles), np.sin(angles)
    return (
        np.concatenate([cosine, cosine], axis=1).astype(np.float32),
        np.concatenate([-sine, sine], axis=1).astype(np.float32),
    )


def nt_dot(a, b):
    return lax.dot_general(a, b, (((1,), (1,)), ((), ())), preferred_element_type=jnp.float32)


def project_kernel(
    store_ref, owner_ref, new_ref, kw_ref, vw_ref,
    routed_ref, fresh_ref,
    xs, wl, gathered, partial, received, squares, onehot, outgoing, by_y, by_z,
    core_s, core_r, z_s, z_r, y_s, y_r, sum_s, sum_r, sq_s, sq_r, ry_s, ry_r, rz_s, rz_r,
):
    seq = lax.axis_index("seq")
    head = lax.axis_index("head")
    z, y = lax.div(seq, NY), lax.rem(seq, NY)
    x, c = lax.div(head, 2), lax.rem(head, 2)
    other = head + 1 - 2 * c

    def zp(delta):
        return lax.rem(z + delta + NZ, NZ)

    def yp(delta):
        return lax.rem(y + delta + NY, NY)

    def remote(src, dst, send_sem, recv_sem, to_seq, to_head):
        return pltpu.make_async_remote_copy(
            src_ref=src, dst_ref=dst, send_sem=send_sem, recv_sem=recv_sem,
            device_id=(to_seq, to_head), device_id_type=MESH,
        )

    sends = []

    def start(copy):
        copy.start()
        sends.append(copy)

    barrier = pltpu.get_barrier_semaphore()
    peers = [(seq, lax.rem(head + i, 2 * NX)) for i in range(1, 2 * NX)]
    peers += [(z * NY + yp(i), head) for i in range(1, NY)]
    peers += [(zp(i) * NY + y, head) for i in range(1, NZ)]
    for peer in peers:
        pl.semaphore_signal(barrier, inc=1, device_id=peer, device_id_type=MESH)

    own = pl.ds(pl.multiple_of(c * FEAT, FEAT), FEAT)
    theirs = pl.ds(pl.multiple_of((1 - c) * FEAT, FEAT), FEAT)
    wl[0] = kw_ref[...]
    wl[1] = vw_ref[...]
    gathered[z, y, :, own] = wl[c]
    xs[:STORED, own] = store_ref[...]
    xs[STORED:, own] = new_ref[...]
    pl.semaphore_wait(barrier, len(peers))

    start(remote(wl.at[1 - c], gathered.at[z, y, :, own], core_s.at[0], core_r.at[0], seq, other))
    start(remote(xs.at[:, own], xs.at[:, own], core_s.at[1], core_r.at[1], seq, other))
    remote(
        wl.at[1 - c], gathered.at[z, y, :, theirs], core_s.at[0], core_r.at[0], seq, other
    ).wait_recv()

    def z_region(flow, chunk):
        if flow == 0:
            return gathered.at[chunk, y, :, :SPLIT]
        return gathered.at[chunk, :, :, SPLIT:]

    def z_target(d):
        return zp(1 if d == 0 else -1) * NY + y

    def z_chunk(d, t):
        return zp(-t if d == 0 else t)

    def z_send(flow, d, t):
        region = z_region(flow, z_chunk(d, t - 1))
        start(remote(region, region, z_s.at[flow, d, t], z_r.at[flow, d, t], z_target(d), head))

    def z_wait(flow, d, t):
        region = z_region(flow, z_chunk(d, t))
        remote(region, region, z_s.at[flow, d, t], z_r.at[flow, d, t], z_target(d), head).wait_recv()

    def z_has(flow, d, t):
        return t < NZ // 2 or (t == NZ // 2 and flow == d)

    def y_target(d):
        return z * NY + yp(1 if d == 0 else -1)

    def y_copy(index, chunk, lo, hi, stage, d, delta):
        region = gathered.at[chunk, yp(delta), :, lo:hi]
        return remote(
            region, region, y_s.at[index, stage, d], y_r.at[index, stage, d], y_target(d), head
        )

    def y_one(index, chunk, lo, hi):
        for d in (0, 1):
            start(y_copy(index, chunk, lo, hi, 0, d, 0))

    def y_two(index, chunk, lo, hi):
        mid = (lo + hi) // 2
        y_copy(index, chunk, lo, hi, 0, 0, -1).wait_recv()
        start(y_copy(index, chunk, lo, mid, 1, 0, -1))
        y_copy(index, chunk, lo, hi, 0, 1, 1).wait_recv()
        start(y_copy(index, chunk, mid, hi, 1, 1, 1))

    def y_end(index, chunk, lo, hi):
        mid = (lo + hi) // 2
        y_copy(index, chunk, lo, mid, 1, 0, 2).wait_recv()
        y_copy(index, chunk, mid, hi, 1, 1, 2).wait_recv()

    def chunks_of(t):
        if t == 0:
            return [(0, z)]
        return [(2 * t + d, z_chunk(d, t)) for d in (0, 1) if z_has(0, d, t)]

    for d in (0, 1):
        z_send(0, d, 1)
    y_one(1, z, SPLIT, CHIP_FEAT)
    y_one(0, z, 0, SPLIT)

    ones = jnp.ones((8, 256), jnp.bfloat16)
    total = jnp.zeros((8, ROWS), jnp.float32)
    for piece in range(FEAT // 256):
        at = pl.ds(piece * 256, 256)
        block = jnp.concatenate([store_ref[:, at], new_ref[:, at]], axis=0).astype(jnp.float32)
        square = block * block
        high = square.astype(jnp.bfloat16)
        low = (square - high.astype(jnp.float32)).astype(jnp.bfloat16)
        total += nt_dot(ones, high) + nt_dot(ones, low)
    squares[head] = total
    for i in range(1, 2 * NX):
        to = lax.rem(head + i, 2 * NX)
        start(remote(squares.at[head], squares.at[head], sq_s.at[to], sq_r.at[head], seq, to))

    y_two(1, z, SPLIT, CHIP_FEAT)

    owner_row = owner_ref[...]
    owner_lanes = jnp.broadcast_to(owner_row.astype(jnp.float32), (STORED, STORED))
    earlier = lax.broadcasted_iota(jnp.int32, (STORED, STORED), 0) < lax.broadcasted_iota(
        jnp.int32, (STORED, STORED), 1
    )
    same = jnp.where(earlier & (owner_lanes.T == owner_lanes), 1.0, 0.0)
    rank = jnp.sum(same, axis=0, keepdims=True).astype(jnp.int32)
    owner_z = lax.shift_right_logical(owner_row, 2)
    owner_y = lax.bitwise_and(owner_row, 3)
    slot = (owner_y * NZ + owner_z) * CAP + rank
    onehot[...] = jnp.where(
        lax.broadcasted_iota(jnp.int32, (HIST, STORED), 0) == slot, 1.0, 0.0
    ).astype(jnp.bfloat16)

    remote(xs.at[:, theirs], xs.at[:, theirs], core_s.at[1], core_r.at[1], seq, other).wait_recv()

    def send_sum(chunk):
        to = lax.div(chunk, 2)
        half = lax.rem(chunk, 2)
        result = nt_dot(gathered[chunk].reshape(4 * 16, CHIP_FEAT), xs[...]).astype(jnp.bfloat16)
        partial[chunk] = result

        @pl.when(to == head)
        def _():
            received[x, c, half] = result

        @pl.when(to != head)
        def _():
            remote(
                partial.at[chunk], received.at[x, c, half],
                sum_s.at[chunk], sum_r.at[x, c, half], seq, to,
            ).start()

    last = NZ // 2
    for s in range(1, last + 3):
        if s <= last:
            for d in (0, 1):
                if z_has(0, d, s):
                    z_wait(0, d, s)
                    if z_has(0, d, s + 1):
                        z_send(0, d, s + 1)
                    y_one(2 * s + d, z_chunk(d, s), 0, SPLIT)
        if s == 1:
            y_end(1, z, SPLIT, CHIP_FEAT)
            for d in (0, 1):
                z_send(1, d, 1)
        elif s - 1 <= last:
            for d in (0, 1):
                if z_has(1, d, s - 1):
                    z_wait(1, d, s - 1)
                    if z_has(1, d, s):
                        z_send(1, d, s)
        if s - 1 <= last:
            for index, chunk in chunks_of(s - 1):
                y_two(index, chunk, 0, SPLIT)
        if s >= 2:
            for index, chunk in chunks_of(s - 2):
                y_end(index, chunk, 0, SPLIT)
                send_sum(chunk)

    for i in range(1, 2 * NX):
        frm = lax.rem(head + i, 2 * NX)
        remote(squares.at[frm], squares.at[frm], sq_s.at[frm], sq_r.at[frm], seq, frm).wait_recv()
    sums = jnp.sum(jnp.sum(squares[...], axis=0), axis=0, keepdims=True) * 0.125
    scale = lax.rsqrt(sums / D + 1e-05)
    for i in range(1, 2 * NX):
        frm = lax.rem(head + i, 2 * NX)
        fx, fc = lax.div(frm, 2), lax.rem(frm, 2)
        for half in (0, 1):
            remote(
                received.at[fx, fc, half], received.at[fx, fc, half],
                sum_s.at[0], sum_r.at[fx, fc, half], seq, frm,
            ).wait_recv()
    kinds = []
    for kind in (0, 1):
        summed = jnp.zeros((HD, ROWS), jnp.float32)
        for fx in range(NX):
            summed += received[fx, kind].reshape(HD, ROWS).astype(jnp.float32)
        scaled = summed * scale
        fresh_ref[kind] = scaled[:, STORED:]
        kinds.append(nt_dot(onehot[...], scaled[:, :STORED].astype(jnp.bfloat16)))
    filled = jnp.sum(onehot[...].astype(jnp.float32), axis=1, keepdims=True)
    keys = kinds[0] + (1.0 - filled) * EMPTY
    slots = jnp.concatenate(
        [keys.reshape(SESS, CAP, HD), kinds[1].reshape(SESS, CAP, HD)], axis=1
    )
    outgoing[...] = slots.astype(jnp.bfloat16).reshape(NY, NZ, 2 * CAP, HD)

    for i in (2, 1, 3):
        to = yp(i)
        start(remote(outgoing.at[to], by_y.at[y], ry_s.at[to], ry_r.at[y], z * NY + to, head))
    by_y[y] = outgoing[y]
    for i in (1, 3, 2):
        frm = yp(i)
        remote(outgoing.at[frm], by_y.at[frm], ry_s.at[frm], ry_r.at[frm], z * NY + frm, head).wait_recv()
    order = [8, 7, 9, 6, 10, 5, 11, 4, 12, 3, 13, 2, 14, 1, 15]
    for i in order:
        to = zp(i)
        start(remote(by_y.at[:, to], by_z.at[z], rz_s.at[to], rz_r.at[z], to * NY + y, head))
    by_z[z] = by_y[:, z]
    for i in reversed(order):
        frm = zp(i)
        remote(by_y.at[:, frm], by_z.at[frm], rz_s.at[frm], rz_r.at[frm], frm * NY + y, head).wait_recv()
    routed_ref[...] = by_z[...].reshape(SESS, 2 * CAP, HD)

    for copy in sends:
        copy.wait_send()
    for chunk in range(NZ):
        @pl.when(chunk // 2 != head)
        def _(chunk=chunk):
            remote(
                partial.at[chunk], received.at[x, c, 0],
                sum_s.at[chunk], sum_r.at[x, c, 0], seq, other,
            ).wait_send()


def project(store_hidden, owner_row, new_hidden, key_columns, value_columns):
    dma = pltpu.SemaphoreType.DMA
    vmem = pl.BlockSpec(memory_space=pltpu.VMEM)
    return pl.pallas_call(
        project_kernel,
        out_shape=(
            jax.ShapeDtypeStruct((SESS, 2 * CAP, HD), jnp.bfloat16),
            jax.ShapeDtypeStruct((2, HD, TURN), jnp.float32),
        ),
        in_specs=[vmem] * 5,
        out_specs=(vmem, vmem),
        scratch_shapes=[
            pltpu.VMEM((ROWS, CHIP_FEAT), jnp.bfloat16),
            pltpu.VMEM((2, 16, FEAT), jnp.bfloat16),
            pltpu.VMEM((NZ, NY, 16, CHIP_FEAT), jnp.bfloat16),
            pltpu.VMEM((NZ, 64, ROWS), jnp.bfloat16),
            pltpu.VMEM((NX, 2, 2, 64, ROWS), jnp.bfloat16),
            pltpu.VMEM((2 * NX, 8, ROWS), jnp.float32),
            pltpu.VMEM((HIST, STORED), jnp.bfloat16),
            pltpu.VMEM((NY, NZ, 2 * CAP, HD), jnp.bfloat16),
            pltpu.VMEM((NY, NZ, 2 * CAP, HD), jnp.bfloat16),
            pltpu.VMEM((NZ, NY, 2 * CAP, HD), jnp.bfloat16),
            dma((2,)), dma((2,)),
            dma((2, 2, 9)), dma((2, 2, 9)),
            dma((18, 2, 2)), dma((18, 2, 2)),
            dma((NZ,)), dma((NX, 2, 2)),
            dma((2 * NX,)), dma((2 * NX,)),
            dma((NY,)), dma((NY,)),
            dma((NZ,)), dma((NZ,)),
        ],
        compiler_params=pltpu.CompilerParams(
            collective_id=0, has_side_effects=True, vmem_limit_bytes=48 * 1024 * 1024
        ),
        name="project_rows",
    )(store_hidden, owner_row, new_hidden, key_columns, value_columns)


def attend_kernel(
    turn_ref, rows_ref, fresh_ref, query_ref, cos_ref, sin_ref, out_ref, key_ref, value_ref
):
    def rotate(values, cosine, sine):
        return values * cosine + pltpu.roll(values, HD // 2, 1) * sine

    rows = rows_ref[...].astype(jnp.float32)
    sent_keys = rows[:, :CAP].reshape(HIST, HD)
    sent_values = rows[:, CAP:].reshape(HIST, HD)
    valid = jnp.abs(sent_keys) < EMPTY_TEST
    sent_keys = jnp.where(valid, sent_keys, 0.0).astype(jnp.bfloat16)
    marks = jnp.where(valid, 1.0, 0.0)
    row_at = lax.broadcasted_iota(jnp.int32, (HIST, HIST), 0)
    lane_at = lax.broadcasted_iota(jnp.int32, (HIST, HIST), 1)
    before = jnp.where(lane_at < row_at, 1.0, 0.0).astype(jnp.bfloat16)
    position = jnp.dot(before, marks.astype(jnp.bfloat16), preferred_element_type=jnp.float32)
    position = jnp.where(valid, position, -1.0).T[:1].astype(jnp.int32)
    place = jnp.where(row_at == position, 1.0, 0.0).astype(jnp.bfloat16)
    history = jnp.dot(
        place,
        jnp.concatenate([sent_keys, sent_values.astype(jnp.bfloat16)], axis=1),
        preferred_element_type=jnp.float32,
    )
    length = jnp.sum(marks[:, :1]).astype(jnp.int32)
    turn = turn_ref[0]

    key_ref[0, :HIST] = rotate(history[:, :HD], cos_ref[:HIST], sin_ref[:HIST]).astype(jnp.bfloat16)
    value_ref[0, :HIST] = history[:, HD:].astype(jnp.bfloat16)
    cosine = cos_ref[pl.ds(length, TURN), :]
    sine = sin_ref[pl.ds(length, TURN), :]
    live = lax.broadcasted_iota(jnp.int32, (TURN, HD), 0) < turn
    key_ref[0, HIST:] = jnp.where(live, rotate(fresh_ref[0].T, cosine, sine), 0.0).astype(jnp.bfloat16)
    value_ref[0, HIST:] = jnp.where(live, fresh_ref[1].T, 0.0).astype(jnp.bfloat16)

    keys = key_ref[0]
    values = value_ref[0]
    slot_at = lax.broadcasted_iota(jnp.int32, (TURN, CACHE), 0)
    cache_at = lax.broadcasted_iota(jnp.int32, (TURN, CACHE), 1)
    allowed = (cache_at < length) | ((cache_at >= HIST) & (cache_at - HIST <= slot_at))
    for group in range(QH // KVH):
        at = pl.ds(group * HD, HD)
        query = rotate(query_ref[:, at].astype(jnp.float32), cosine, sine).astype(jnp.bfloat16)
        scores = nt_dot(query, keys) * (1.0 / math.sqrt(HD))
        scores = jnp.where(allowed, scores, -jnp.inf)
        exponent = jnp.exp(scores - jnp.max(scores, axis=1, keepdims=True))
        weights = (exponent / jnp.sum(exponent, axis=1, keepdims=True)).astype(jnp.bfloat16)
        result = jnp.dot(weights, values, preferred_element_type=jnp.float32)
        out_ref[:, at] = jnp.where(live, result, 0.0).astype(jnp.bfloat16)


def attend(turn_length, rows, fresh, queries):
    cosine, sine = rotation_tables()
    vmem = pl.BlockSpec(memory_space=pltpu.VMEM)
    return pl.pallas_call(
        attend_kernel,
        out_shape=(
            jax.ShapeDtypeStruct((TURN, QH // KVH * HD), jnp.bfloat16),
            jax.ShapeDtypeStruct((1, CACHE, HD), jnp.bfloat16),
            jax.ShapeDtypeStruct((1, CACHE, HD), jnp.bfloat16),
        ),
        in_specs=[pl.BlockSpec(memory_space=pltpu.SMEM)] + [vmem] * 5,
        out_specs=(vmem, vmem, vmem),
        compiler_params=pltpu.CompilerParams(vmem_limit_bytes=48 * 1024 * 1024),
        name="attend_turn",
    )(turn_length, rows, fresh, queries, jnp.asarray(cosine), jnp.asarray(sine))


def local(store_hidden, owner_map, new_hidden, new_lengths, queries, key_weight, value_weight):
    rows, fresh = project(
        store_hidden, owner_map.reshape(1, STORED), new_hidden, key_weight.T, value_weight.T
    )
    return attend(new_lengths, rows, fresh, queries)


def solution(mesh):
    placed = (
        P("seq", "head"),
        P("seq", None),
        P("seq", "head"),
        P("seq"),
        P("seq", "head"),
        P("head", "seq"),
        P("head", "seq"),
    )
    return jax.shard_map(
        local,
        mesh=mesh,
        in_specs=placed,
        out_specs=(P("seq", "head"), P("seq", None, "head"), P("seq", None, "head")),
        check_vma=False,
    )
```

```python
import functools
import math

import jax
import jax.numpy as jnp
import numpy as np
from jax import lax
from jax.experimental import pallas as pl
from jax.experimental.pallas import tpu as pltpu
from jax.sharding import PartitionSpec as P

D = 8192
QH = 64
KVH = 8
HD = 128
NZ = 16
NY = 4
NX = 4
STORED = 256
TURN = 128
ROWS = STORED + TURN
CAP = 8
SESS = NZ * NY
HIST = SESS * CAP
CACHE = HIST + TURN
FEAT = D // (2 * NX)
CHIP_FEAT = 2 * FEAT
SPLIT = 1280
EMPTY = float(2.0**100)
EMPTY_TEST = float(2.0**50)
MESH = pl.DeviceIdType.MESH
rope_base = 500000.0


def rotation_tables():
    half_index = np.arange(HD // 2, dtype=np.float64)
    inverse = 1.0 / np.power(rope_base, 2.0 * half_index / HD)
    wavelength = 2.0 * np.pi / inverse
    smooth = (8192.0 / wavelength - 1.0) / 3.0
    mixed = (1.0 - smooth) * inverse / 8.0 + smooth * inverse
    frequency = np.where(
        wavelength < 2048.0, inverse, np.where(wavelength > 8192.0, inverse / 8.0, mixed)
    )
    angles = np.arange(CACHE, dtype=np.float64)[:, None] * frequency[None, :]
    cosine, sine = np.cos(angles), np.sin(angles)
    return (
        np.concatenate([cosine, cosine], axis=1).astype(np.float32),
        np.concatenate([-sine, sine], axis=1).astype(np.float32),
    )


def nt_dot(a, b):
    return lax.dot_general(a, b, (((1,), (1,)), ((), ())), preferred_element_type=jnp.float32)


def project_kernel(
    store_ref, owner_ref, new_ref, kw_ref, vw_ref,
    routed_ref, fresh_ref,
    xs, owners, gathered, partial, received, squares, onehot, empties, outgoing, by_y, by_z,
    in_s, core_s, core_r, z_s, z_r, y_s, y_r, sum_s, sum_r, sq_s, sq_r, ry_s, ry_r, rz_s, rz_r,
):
    seq = lax.axis_index("seq")
    head = lax.axis_index("head")
    z, y = lax.div(seq, NY), lax.rem(seq, NY)
    x, c = lax.div(head, 2), lax.rem(head, 2)
    other = head + 1 - 2 * c

    def zp(delta):
        return lax.rem(z + delta + NZ, NZ)

    def yp(delta):
        return lax.rem(y + delta + NY, NY)

    def remote(src, dst, send_sem, recv_sem, to_seq, to_head):
        return pltpu.make_async_remote_copy(
            src_ref=src, dst_ref=dst, send_sem=send_sem, recv_sem=recv_sem,
            device_id=(to_seq, to_head), device_id_type=MESH,
        )

    sends = []

    def start(copy):
        copy.start()
        sends.append(copy)

    barrier = pltpu.get_barrier_semaphore()
    peers = [(z * NY + yp(i), head) for i in (1, -1)]
    peers += [(zp(i) * NY + y, head) for i in (1, -1)]
    peers += [(seq, lax.rem(head + i, 2 * NX)) for i in range(1, 2 * NX)]
    for peer in peers:
        pl.semaphore_signal(barrier, inc=1, device_id=peer, device_id_type=MESH)

    own = pl.ds(pl.multiple_of(c * FEAT, FEAT), FEAT)
    theirs = pl.ds(pl.multiple_of((1 - c) * FEAT, FEAT), FEAT)
    mine = gathered.at[z, y, :, own]

    def own_weights(ref):
        return pltpu.make_async_copy(ref, mine, in_s.at[0])

    def their_weights(ref):
        return remote(ref, mine, core_s.at[0], core_r.at[0], seq, other)

    @pl.when(c == 0)
    def _():
        own_weights(kw_ref).start()

    @pl.when(c == 1)
    def _():
        own_weights(vw_ref).start()

    store_in = pltpu.make_async_copy(store_ref, xs.at[:STORED, own], in_s.at[1])
    new_in = pltpu.make_async_copy(new_ref, xs.at[STORED:, own], in_s.at[2])
    owner_in = pltpu.make_async_copy(owner_ref, owners, in_s.at[3])
    for copy in (store_in, new_in, owner_in):
        copy.start()
    pl.semaphore_wait(barrier, len(peers))

    @pl.when(c == 0)
    def _():
        their_weights(vw_ref).start()

    @pl.when(c == 1)
    def _():
        their_weights(kw_ref).start()

    start(remote(store_ref, xs.at[:STORED, own], core_s.at[1], core_r.at[1], seq, other))
    start(remote(new_ref, xs.at[STORED:, own], core_s.at[2], core_r.at[2], seq, other))
    own_weights(kw_ref).wait()
    remote(
        kw_ref, gathered.at[z, y, :, theirs], core_s.at[0], core_r.at[0], seq, other
    ).wait_recv()

    flows = [
        (0, 0, SPLIT, 0, 0),
        (0, SPLIT, CHIP_FEAT, 0, 0),
        (-1, SPLIT, CHIP_FEAT, 1, 1),
        (1, SPLIT, CHIP_FEAT, 1, 1),
        (2, SPLIT, CHIP_FEAT, 1, 2),
    ]
    far = NZ // 2

    def z_chunk(d, t):
        return zp(-t if d == 0 else t)

    def z_copy(flow, d, t, chunk):
        delta, lo, hi = flows[flow][:3]
        region = gathered.at[chunk, yp(delta), :, lo:hi]
        return remote(
            region, region, z_s.at[flow, d, t], z_r.at[flow, d, t],
            zp(1 if d == 0 else -1) * NY + y, head,
        )

    def z_has(flow, d, t):
        return t < far or (t == far and flows[flow][3] == d)

    def z_first(flow):
        for d in (0, 1):
            start(z_copy(flow, d, 1, z))

    def z_pass(flow, t):
        for d in (0, 1):
            if z_has(flow, d, t):
                chunk = z_chunk(d, t)
                z_copy(flow, d, t, chunk).wait_recv()
                if z_has(flow, d, t + 1):
                    start(z_copy(flow, d, t + 1, chunk))

    def y_copy(index, chunk, lo, hi, stage, d, delta):
        region = gathered.at[chunk, yp(delta), :, lo:hi]
        return remote(
            region, region, y_s.at[index, stage, d], y_r.at[index, stage, d],
            z * NY + yp(1 if d == 0 else -1), head,
        )

    def y_one(index, chunk, lo, hi):
        for d in (0, 1):
            start(y_copy(index, chunk, lo, hi, 0, d, 0))

    def half_way(lo, hi):
        return lo + (hi - lo) // 256 * 128

    def y_two(index, chunk, lo, hi, d):
        mid = half_way(lo, hi)
        y_copy(index, chunk, lo, hi, 0, d, -1 if d == 0 else 1).wait_recv()
        if d == 0:
            start(y_copy(index, chunk, lo, mid, 1, 0, -1))
        else:
            start(y_copy(index, chunk, mid, hi, 1, 1, 1))

    def y_end(index, chunk, lo, hi):
        mid = half_way(lo, hi)
        y_copy(index, chunk, lo, mid, 1, 0, 2).wait_recv()
        y_copy(index, chunk, mid, hi, 1, 1, 2).wait_recv()

    def chunks_of(t):
        if t == 0:
            return [(0, z)]
        return [(2 * t + d, z_chunk(d, t)) for d in (0, 1) if z_has(0, d, t)]

    def sum_squares():
        store_in.wait()
        new_in.wait()
        ones = jnp.ones((8, 256), jnp.bfloat16)
        total = jnp.zeros((8, ROWS), jnp.float32)
        for piece in range(FEAT // 256):
            at = pl.ds(pl.multiple_of(c * FEAT + piece * 256, 256), 256)
            block = xs[:, at].astype(jnp.float32)
            square = block * block
            high = square.astype(jnp.bfloat16)
            low = (square - high.astype(jnp.float32)).astype(jnp.bfloat16)
            total += nt_dot(ones, high) + nt_dot(ones, low)
        squares[head] = total
        for i in range(1, 2 * NX):
            to = lax.rem(head + i, 2 * NX)
            start(remote(squares.at[head], squares.at[head], sq_s.at[to], sq_r.at[head], seq, to))

    def find_slots():
        owner_in.wait()
        owner_row = owners[...]
        owner_lanes = jnp.broadcast_to(owner_row.astype(jnp.float32), (STORED, STORED))
        earlier = lax.broadcasted_iota(jnp.int32, (STORED, STORED), 0) < lax.broadcasted_iota(
            jnp.int32, (STORED, STORED), 1
        )
        same = jnp.where(earlier & (owner_lanes.T == owner_lanes), 1.0, 0.0)
        rank = jnp.sum(same, axis=0, keepdims=True).astype(jnp.int32)
        owner_z = lax.shift_right_logical(owner_row, 2)
        owner_y = lax.bitwise_and(owner_row, 3)
        slot = (owner_y * NZ + owner_z) * CAP + rank
        hot = jnp.where(lax.broadcasted_iota(jnp.int32, (HIST, STORED), 0) == slot, 1.0, 0.0)
        onehot[...] = hot.astype(jnp.bfloat16)
        filled = jnp.sum(hot, axis=1, keepdims=True)
        empties[...] = jnp.broadcast_to((1.0 - filled) * EMPTY, (HIST, HD))

    def take_rows():
        for i, rows in ((1, slice(0, STORED)), (2, slice(STORED, ROWS))):
            region = xs.at[rows, theirs]
            remote(region, region, core_s.at[i], core_r.at[i], seq, other).wait_recv()

    def send_sum(chunk):
        to = lax.div(chunk, 2)
        half = lax.rem(chunk, 2)
        result = nt_dot(gathered[chunk].reshape(4 * 16, CHIP_FEAT), xs[...]).astype(jnp.bfloat16)
        partial[chunk] = result

        @pl.when(to == head)
        def _():
            received[x, c, half] = result

        @pl.when(to != head)
        def _():
            remote(
                partial.at[chunk], received.at[x, c, half],
                sum_s.at[chunk], sum_r.at[x, c, half], seq, to,
            ).start()

    z_first(0)
    z_first(1)
    y_one(1, z, SPLIT, CHIP_FEAT)
    y_one(0, z, 0, SPLIT)
    for d in (0, 1):
        y_two(1, z, SPLIT, CHIP_FEAT, d)
        z_first(2 + d)

    for s in range(1, far + 3):
        if s <= far:
            z_pass(0, s)
            z_pass(1, s)
            for index, chunk in chunks_of(s):
                y_one(index, chunk, 0, SPLIT)
        if 1 <= s - 1 <= far:
            z_pass(2, s - 1)
            z_pass(3, s - 1)
        if s == 1:
            y_end(1, z, SPLIT, CHIP_FEAT)
            z_first(4)
        elif 1 <= s - 2 <= far:
            z_pass(4, s - 2)
        if s == 1:
            sum_squares()
        if s - 1 <= far:
            for index, chunk in chunks_of(s - 1):
                for d in (0, 1):
                    y_two(index, chunk, 0, SPLIT, d)
        if s == 2:
            find_slots()
            take_rows()
        if s >= 2:
            for index, chunk in chunks_of(s - 2):
                y_end(index, chunk, 0, SPLIT)
                send_sum(chunk)

    for i in range(1, 2 * NX):
        frm = lax.rem(head + i, 2 * NX)
        remote(squares.at[frm], squares.at[frm], sq_s.at[frm], sq_r.at[frm], seq, frm).wait_recv()
    sums = jnp.sum(jnp.sum(squares[...], axis=0), axis=0, keepdims=True) * 0.125
    scale = lax.rsqrt(sums / D + 1e-05)
    for i in range(1, 2 * NX):
        frm = lax.rem(head + i, 2 * NX)
        fx, fc = lax.div(frm, 2), lax.rem(frm, 2)
        for half in (0, 1):
            remote(
                received.at[fx, fc, half], received.at[fx, fc, half],
                sum_s.at[0], sum_r.at[fx, fc, half], seq, frm,
            ).wait_recv()
    kinds = []
    for kind in (0, 1):
        summed = jnp.zeros((HD, ROWS), jnp.float32)
        for fx in range(NX):
            summed += received[fx, kind].reshape(HD, ROWS).astype(jnp.float32)
        scaled = summed * scale
        fresh_ref[kind] = scaled[:, STORED:]
        kinds.append(nt_dot(onehot[...], scaled[:, :STORED].astype(jnp.bfloat16)))
    keys = kinds[0] + empties[...]
    slots = jnp.concatenate(
        [keys.reshape(SESS, CAP, HD), kinds[1].reshape(SESS, CAP, HD)], axis=1
    )
    outgoing[...] = slots.astype(jnp.bfloat16).reshape(NY, NZ, 2 * CAP, HD)

    for i in (2, 1, 3):
        to = yp(i)
        start(remote(outgoing.at[to], by_y.at[y], ry_s.at[to], ry_r.at[y], z * NY + to, head))
    by_y[y] = outgoing[y]
    for i in (1, 3, 2):
        frm = yp(i)
        remote(outgoing.at[frm], by_y.at[frm], ry_s.at[frm], ry_r.at[frm], z * NY + frm, head).wait_recv()
    order = [8, 7, 9, 6, 10, 5, 11, 4, 12, 3, 13, 2, 14, 1, 15]
    for i in order:
        to = zp(i)
        start(remote(by_y.at[:, to], by_z.at[z], rz_s.at[to], rz_r.at[z], to * NY + y, head))
    by_z[z] = by_y[:, z]
    for i in reversed(order):
        frm = zp(i)
        remote(by_y.at[:, frm], by_z.at[frm], rz_s.at[frm], rz_r.at[frm], frm * NY + y, head).wait_recv()
    routed_ref[...] = by_z[...].reshape(SESS, 2 * CAP, HD)

    their_weights(kw_ref).wait_send()
    for copy in sends:
        copy.wait_send()
    for chunk in range(NZ):
        @pl.when(chunk // 2 != head)
        def _(chunk=chunk):
            remote(
                partial.at[chunk], received.at[x, c, 0],
                sum_s.at[chunk], sum_r.at[x, c, 0], seq, other,
            ).wait_send()


def project(store_hidden, owner_row, new_hidden, key_columns, value_columns):
    dma = pltpu.SemaphoreType.DMA
    vmem = pl.BlockSpec(memory_space=pltpu.VMEM)
    return pl.pallas_call(
        project_kernel,
        out_shape=(
            jax.ShapeDtypeStruct((SESS, 2 * CAP, HD), jnp.bfloat16),
            jax.ShapeDtypeStruct((2, HD, TURN), jnp.float32),
        ),
        in_specs=[pl.BlockSpec(memory_space=pltpu.HBM)] * 5,
        out_specs=(vmem, vmem),
        scratch_shapes=[
            pltpu.VMEM((ROWS, CHIP_FEAT), jnp.bfloat16),
            pltpu.VMEM((1, STORED), jnp.int32),
            pltpu.VMEM((NZ, NY, 16, CHIP_FEAT), jnp.bfloat16),
            pltpu.VMEM((NZ, 64, ROWS), jnp.bfloat16),
            pltpu.VMEM((NX, 2, 2, 64, ROWS), jnp.bfloat16),
            pltpu.VMEM((2 * NX, 8, ROWS), jnp.float32),
            pltpu.VMEM((HIST, STORED), jnp.bfloat16),
            pltpu.VMEM((HIST, HD), jnp.float32),
            pltpu.VMEM((NY, NZ, 2 * CAP, HD), jnp.bfloat16),
            pltpu.VMEM((NY, NZ, 2 * CAP, HD), jnp.bfloat16),
            pltpu.VMEM((NZ, NY, 2 * CAP, HD), jnp.bfloat16),
            dma((4,)),
            dma((3,)), dma((3,)),
            dma((5, 2, 9)), dma((5, 2, 9)),
            dma((18, 2, 2)), dma((18, 2, 2)),
            dma((NZ,)), dma((NX, 2, 2)),
            dma((2 * NX,)), dma((2 * NX,)),
            dma((NY,)), dma((NY,)),
            dma((NZ,)), dma((NZ,)),
        ],
        compiler_params=pltpu.CompilerParams(
            collective_id=0, has_side_effects=True, vmem_limit_bytes=48 * 1024 * 1024
        ),
        name="project_rows",
    )(store_hidden, owner_row, new_hidden, key_columns, value_columns)


def attend_kernel(
    turn_ref, rows_ref, fresh_ref, query_ref, cos_ref, sin_ref, out_ref, key_ref, value_ref
):
    def rotate(values, cosine, sine):
        return values * cosine + pltpu.roll(values, HD // 2, 1) * sine

    rows = rows_ref[...].astype(jnp.float32)
    sent_keys = rows[:, :CAP].reshape(HIST, HD)
    sent_values = rows[:, CAP:].reshape(HIST, HD)
    valid = jnp.abs(sent_keys) < EMPTY_TEST
    sent_keys = jnp.where(valid, sent_keys, 0.0).astype(jnp.bfloat16)
    marks = jnp.where(valid, 1.0, 0.0)
    row_at = lax.broadcasted_iota(jnp.int32, (HIST, HIST), 0)
    lane_at = lax.broadcasted_iota(jnp.int32, (HIST, HIST), 1)
    before = jnp.where(lane_at < row_at, 1.0, 0.0).astype(jnp.bfloat16)
    position = jnp.dot(before, marks.astype(jnp.bfloat16), preferred_element_type=jnp.float32)
    position = jnp.where(valid, position, -1.0).T[:1].astype(jnp.int32)
    place = jnp.where(row_at == position, 1.0, 0.0).astype(jnp.bfloat16)
    history = jnp.dot(
        place,
        jnp.concatenate([sent_keys, sent_values.astype(jnp.bfloat16)], axis=1),
        preferred_element_type=jnp.float32,
    )
    length = jnp.sum(marks[:, :1]).astype(jnp.int32)
    turn = turn_ref[0]

    key_ref[0, :HIST] = rotate(history[:, :HD], cos_ref[:HIST], sin_ref[:HIST]).astype(jnp.bfloat16)
    value_ref[0, :HIST] = history[:, HD:].astype(jnp.bfloat16)
    cosine = cos_ref[pl.ds(length, TURN), :]
    sine = sin_ref[pl.ds(length, TURN), :]
    live = lax.broadcasted_iota(jnp.int32, (TURN, HD), 0) < turn
    key_ref[0, HIST:] = jnp.where(live, rotate(fresh_ref[0].T, cosine, sine), 0.0).astype(jnp.bfloat16)
    value_ref[0, HIST:] = jnp.where(live, fresh_ref[1].T, 0.0).astype(jnp.bfloat16)

    keys = key_ref[0]
    values = value_ref[0]
    slot_at = lax.broadcasted_iota(jnp.int32, (TURN, CACHE), 0)
    cache_at = lax.broadcasted_iota(jnp.int32, (TURN, CACHE), 1)
    allowed = (cache_at < length) | ((cache_at >= HIST) & (cache_at - HIST <= slot_at))
    for group in range(QH // KVH):
        at = pl.ds(group * HD, HD)
        query = rotate(query_ref[:, at].astype(jnp.float32), cosine, sine).astype(jnp.bfloat16)
        scores = nt_dot(query, keys) * (1.0 / math.sqrt(HD))
        scores = jnp.where(allowed, scores, -jnp.inf)
        exponent = jnp.exp(scores - jnp.max(scores, axis=1, keepdims=True))
        weights = (exponent / jnp.sum(exponent, axis=1, keepdims=True)).astype(jnp.bfloat16)
        result = jnp.dot(weights, values, preferred_element_type=jnp.float32)
        out_ref[:, at] = jnp.where(live, result, 0.0).astype(jnp.bfloat16)


def attend(turn_length, rows, fresh, queries):
    cosine, sine = rotation_tables()
    vmem = pl.BlockSpec(memory_space=pltpu.VMEM)
    return pl.pallas_call(
        attend_kernel,
        out_shape=(
            jax.ShapeDtypeStruct((TURN, QH // KVH * HD), jnp.bfloat16),
            jax.ShapeDtypeStruct((1, CACHE, HD), jnp.bfloat16),
            jax.ShapeDtypeStruct((1, CACHE, HD), jnp.bfloat16),
        ),
        in_specs=[pl.BlockSpec(memory_space=pltpu.SMEM)] + [vmem] * 5,
        out_specs=(vmem, vmem, vmem),
        compiler_params=pltpu.CompilerParams(vmem_limit_bytes=48 * 1024 * 1024),
        name="attend_turn",
    )(turn_length, rows, fresh, queries, jnp.asarray(cosine), jnp.asarray(sine))


def local(store_hidden, owner_map, new_hidden, new_lengths, queries, key_weight, value_weight):
    rows, fresh = project(
        store_hidden, owner_map.reshape(1, STORED), new_hidden, key_weight.T, value_weight.T
    )
    return attend(new_lengths, rows, fresh, queries)


def solution(mesh):
    placed = (
        P("seq", "head"),
        P("seq", None),
        P("seq", "head"),
        P("seq"),
        P("seq", "head"),
        P("head", "seq"),
        P("head", "seq"),
    )
    return jax.shard_map(
        local,
        mesh=mesh,
        in_specs=placed,
        out_specs=(P("seq", "head"), P("seq", None, "head"), P("seq", None, "head")),
        check_vma=False,
    )
```

```python
import functools
import math

import jax
import jax.numpy as jnp
import numpy as np
from jax import lax
from jax.experimental import pallas as pl
from jax.experimental.pallas import tpu as pltpu
from jax.sharding import PartitionSpec as P

D = 8192
QH = 64
KVH = 8
HD = 128
NZ = 16
NY = 4
NX = 4
STORED = 256
TURN = 128
ROWS = STORED + TURN
CAP = 8
SESS = NZ * NY
HIST = SESS * CAP
CACHE = HIST + TURN
FEAT = D // (2 * NX)
CHIP_FEAT = 2 * FEAT
SPLIT = 1664
LAG1 = 2.7
LAG2 = 5.4
EMPTY = float(2.0**100)
EMPTY_TEST = float(2.0**50)
MESH = pl.DeviceIdType.MESH
rope_base = 500000.0


def rotation_tables():
    half_index = np.arange(HD // 2, dtype=np.float64)
    inverse = 1.0 / np.power(rope_base, 2.0 * half_index / HD)
    wavelength = 2.0 * np.pi / inverse
    smooth = (8192.0 / wavelength - 1.0) / 3.0
    mixed = (1.0 - smooth) * inverse / 8.0 + smooth * inverse
    frequency = np.where(
        wavelength < 2048.0, inverse, np.where(wavelength > 8192.0, inverse / 8.0, mixed)
    )
    angles = np.arange(CACHE, dtype=np.float64)[:, None] * frequency[None, :]
    cosine, sine = np.cos(angles), np.sin(angles)
    return (
        np.concatenate([cosine, cosine], axis=1).astype(np.float32),
        np.concatenate([-sine, sine], axis=1).astype(np.float32),
    )


def nt_dot(a, b):
    return lax.dot_general(a, b, (((1,), (1,)), ((), ())), preferred_element_type=jnp.float32)


def project_kernel(
    store_ref, owner_ref, new_ref, kw_ref, vw_ref,
    routed_ref, fresh_ref,
    xs, owners, gathered, partial, received, squares, onehot, empties, fresh, outgoing, by_y, by_z,
    in_s, out_s, core_s, core_r, z_s, z_r, y_s, y_r, sum_s, sum_r, sq_s, sq_r, ry_s, ry_r, rz_s, rz_r,
):
    seq = lax.axis_index("seq")
    head = lax.axis_index("head")
    z, y = lax.div(seq, NY), lax.rem(seq, NY)
    x, c = lax.div(head, 2), lax.rem(head, 2)
    other = head + 1 - 2 * c

    def zp(delta):
        return lax.rem(z + delta + NZ, NZ)

    def yp(delta):
        return lax.rem(y + delta + NY, NY)

    def remote(src, dst, send_sem, recv_sem, to_seq, to_head):
        return pltpu.make_async_remote_copy(
            src_ref=src, dst_ref=dst, send_sem=send_sem, recv_sem=recv_sem,
            device_id=(to_seq, to_head), device_id_type=MESH,
        )

    clock = [0.0]
    sends = []

    def start(copy):
        copy.start()
        sends.append((clock[0], copy))

    def drain(age):
        while sends and sends[0][0] <= clock[0] - age:
            sends.pop(0)[1].wait_send()

    barrier = pltpu.get_barrier_semaphore()
    peers = [(z * NY + yp(i), head) for i in (1, -1)]
    peers += [(zp(i) * NY + y, head) for i in (1, -1)]
    peers += [(seq, lax.rem(head + i, 2 * NX)) for i in range(1, 2 * NX)]
    for peer in peers:
        pl.semaphore_signal(barrier, inc=1, device_id=peer, device_id_type=MESH)

    own = pl.ds(pl.multiple_of(c * FEAT, FEAT), FEAT)
    theirs = pl.ds(pl.multiple_of((1 - c) * FEAT, FEAT), FEAT)
    mine = gathered.at[z, 0, :, own]

    def own_weights(ref):
        return pltpu.make_async_copy(ref, mine, in_s.at[0])

    def their_weights(ref):
        return remote(ref, mine, core_s.at[0], core_r.at[0], seq, other)

    @pl.when(c == 0)
    def _():
        own_weights(kw_ref).start()

    @pl.when(c == 1)
    def _():
        own_weights(vw_ref).start()

    store_in = pltpu.make_async_copy(store_ref, xs.at[:STORED, own], in_s.at[1])
    new_in = pltpu.make_async_copy(new_ref, xs.at[STORED:, own], in_s.at[2])
    owner_in = pltpu.make_async_copy(owner_ref, owners, in_s.at[3])
    for copy in (store_in, new_in, owner_in):
        copy.start()
    pl.semaphore_wait(barrier, len(peers))

    @pl.when(c == 0)
    def _():
        their_weights(vw_ref).start()

    @pl.when(c == 1)
    def _():
        their_weights(kw_ref).start()

    own_weights(kw_ref).wait()
    remote(
        kw_ref, gathered.at[z, 0, :, theirs], core_s.at[0], core_r.at[0], seq, other
    ).wait_recv()

    def z_region(way, chunk):
        if way == 0:
            return gathered.at[chunk, 0]
        return gathered.at[chunk, 1:, :, SPLIT:]

    def z_send(way, m, step):
        region = z_region(way, zp(-m))
        at = m + step + NZ // 2
        start(remote(region, region, z_s.at[way, at], z_r.at[way, at], zp(step) * NY + y, head))

    def z_take(way, m):
        region = z_region(way, zp(-m))
        at = m + NZ // 2
        remote(region, region, z_s.at[way, at], z_r.at[way, at], seq, head).wait_recv()

    def onward(way, m):
        if m == 0:
            return [1, -1]
        sign = 1 if m > 0 else -1
        last = NZ // 2 if sign == (1 if way == 0 else -1) else NZ // 2 - 1
        return [sign] if abs(m) < last else []

    def half_way(lo, hi):
        return lo + (hi - lo) // 256 * 128

    def y_piece(index, stage, d, src, dst):
        return remote(
            src, dst, y_s.at[index, stage, d], y_r.at[index, stage, d],
            z * NY + yp(1 if d == 0 else -1), head,
        )

    def y_one(index, chunk, lo, hi):
        for d in (0, 1):
            start(y_piece(
                index, 0, d, gathered.at[chunk, 0, :, lo:hi], gathered.at[chunk, 3 - 2 * d, :, lo:hi]
            ))

    def y_two(index, chunk, lo, hi):
        mid = half_way(lo, hi)
        for d in (0, 1):
            whole = gathered.at[chunk, 3 - 2 * d, :, lo:hi]
            y_piece(index, 0, d, whole, whole).wait_recv()
            part = slice(lo, mid) if d == 0 else slice(mid, hi)
            start(y_piece(
                index, 1, d, gathered.at[chunk, 3 - 2 * d, :, part], gathered.at[chunk, 2, :, part]
            ))

    def y_end(index, chunk, lo, hi):
        mid = half_way(lo, hi)
        for d in (0, 1):
            region = gathered.at[chunk, 2, :, lo:mid] if d == 0 else gathered.at[chunk, 2, :, mid:hi]
            y_piece(index, 1, d, region, region).wait_recv()

    def sum_squares():
        store_in.wait()
        new_in.wait()
        ones = jnp.ones((8, 256), jnp.bfloat16)
        total = jnp.zeros((8, ROWS), jnp.float32)
        for piece in range(FEAT // 256):
            at = pl.ds(pl.multiple_of(c * FEAT + piece * 256, 256), 256)
            block = xs[:, at].astype(jnp.float32)
            square = block * block
            high = square.astype(jnp.bfloat16)
            low = (square - high.astype(jnp.float32)).astype(jnp.bfloat16)
            total += nt_dot(ones, high) + nt_dot(ones, low)
        squares[head] = total
        for i in range(1, 2 * NX):
            to = lax.rem(head + i, 2 * NX)
            start(remote(squares.at[head], squares.at[head], sq_s.at[to], sq_r.at[head], seq, to))

    def find_slots():
        owner_in.wait()
        owner_row = owners[...]
        owner_lanes = jnp.broadcast_to(owner_row.astype(jnp.float32), (STORED, STORED))
        earlier = lax.broadcasted_iota(jnp.int32, (STORED, STORED), 0) < lax.broadcasted_iota(
            jnp.int32, (STORED, STORED), 1
        )
        same = jnp.where(earlier & (owner_lanes.T == owner_lanes), 1.0, 0.0)
        rank = jnp.sum(same, axis=0, keepdims=True).astype(jnp.int32)
        owner_z = lax.shift_right_logical(owner_row, 2)
        owner_y = lax.bitwise_and(owner_row, 3)
        slot = (owner_y * NZ + owner_z) * CAP + rank
        hot = jnp.where(lax.broadcasted_iota(jnp.int32, (HIST, STORED), 0) == slot, 1.0, 0.0)
        onehot[...] = hot.astype(jnp.bfloat16)
        filled = jnp.sum(hot, axis=1, keepdims=True)
        empties[...] = jnp.broadcast_to((1.0 - filled) * EMPTY, (HIST, HD))

    def send_rows():
        start(remote(store_ref, xs.at[:STORED, own], core_s.at[1], core_r.at[1], seq, other))
        start(remote(new_ref, xs.at[STORED:, own], core_s.at[2], core_r.at[2], seq, other))

    def take_rows():
        for i, rows in ((1, slice(0, STORED)), (2, slice(STORED, ROWS))):
            region = xs.at[rows, theirs]
            remote(region, region, core_s.at[i], core_r.at[i], seq, other).wait_recv()

    def send_sum(chunk):
        to = lax.div(chunk, 2)
        half = lax.rem(chunk, 2)
        result = nt_dot(gathered[chunk].reshape(4 * 16, CHIP_FEAT), xs[...]).astype(jnp.bfloat16)
        for r in range(NY):
            partial[chunk, yp(r)] = result[r * 16 : (r + 1) * 16]

        @pl.when(to == head)
        def _():
            received[x, c, half] = partial[chunk]

        @pl.when(to != head)
        def _():
            remote(
                partial.at[chunk], received.at[x, c, half],
                sum_s.at[chunk], sum_r.at[x, c, half], seq, to,
            ).start()

    arrives = {0: 0.0}
    todo = [0]
    while todo:
        m = todo.pop(0)
        for step in onward(0, m):
            arrives[m + step] = arrives[m] + 2.6
            todo.append(m + step)
    events = []
    for m, at in sorted(arrives.items(), key=lambda item: (item[1], item[0])):
        twin = m if abs(m) != NZ // 2 else -m
        if m != 0:
            events.append((at, 0, m))
            events.append((at + 5.3, 1, twin))
        events.append((at + LAG1, 2, m))
        events.append((at + LAG2, 3, m))
    events.append((2.4, 4, 0))
    events.append((5.0, 5, 0))
    events.append((3.0, 6, 0))
    events.append((5.1, 7, 0))
    events.append((5.2, 8, 0))

    for step in onward(0, 0):
        z_send(0, 0, step)
    y_one(17, z, SPLIT, CHIP_FEAT)
    send_rows()
    y_one(8, z, 0, SPLIT)
    for at, kind, m in sorted(events):
        clock[0] = at
        drain(6.0)
        chunk = zp(-m)
        index = m + NZ // 2
        if kind == 0:
            z_take(0, m)
            for step in onward(0, m):
                z_send(0, m, step)
            y_one(index, chunk, 0, SPLIT)
        elif kind == 1:
            z_take(1, m)
            for step in onward(1, m):
                z_send(1, m, step)
        elif kind == 2:
            y_two(index, chunk, 0, SPLIT)
        elif kind == 3:
            y_end(index, chunk, 0, SPLIT)
            send_sum(chunk)
        elif kind == 4:
            y_two(17, z, SPLIT, CHIP_FEAT)
        elif kind == 5:
            y_end(17, z, SPLIT, CHIP_FEAT)
            for step in onward(1, 0):
                z_send(1, 0, step)
        elif kind == 6:
            sum_squares()
        elif kind == 7:
            find_slots()
        else:
            take_rows()

    for i in range(1, 2 * NX):
        frm = lax.rem(head + i, 2 * NX)
        remote(squares.at[frm], squares.at[frm], sq_s.at[frm], sq_r.at[frm], seq, frm).wait_recv()
    sums = jnp.sum(jnp.sum(squares[...], axis=0), axis=0, keepdims=True) * 0.125
    scale = lax.rsqrt(sums / D + 1e-05)
    for i in range(1, 2 * NX):
        frm = lax.rem(head + i, 2 * NX)
        fx, fc = lax.div(frm, 2), lax.rem(frm, 2)
        for half in (0, 1):
            remote(
                received.at[fx, fc, half], received.at[fx, fc, half],
                sum_s.at[0], sum_r.at[fx, fc, half], seq, frm,
            ).wait_recv()
    kinds = []
    for kind in (0, 1):
        summed = jnp.zeros((HD, ROWS), jnp.float32)
        for fx in range(NX):
            summed += received[fx, kind].reshape(HD, ROWS).astype(jnp.float32)
        scaled = summed * scale
        fresh[kind] = scaled[:, STORED:]
        kinds.append(nt_dot(onehot[...], scaled[:, :STORED].astype(jnp.bfloat16)))
    keys = kinds[0] + empties[...]
    slots = jnp.concatenate(
        [keys.reshape(SESS, CAP, HD), kinds[1].reshape(SESS, CAP, HD)], axis=1
    )
    outgoing[...] = slots.astype(jnp.bfloat16).reshape(NY, NZ, 2 * CAP, HD)

    for i in (2, 1, 3):
        to = yp(i)
        start(remote(outgoing.at[to], by_y.at[NY - i], ry_s.at[i], ry_r.at[NY - i], z * NY + to, head))
    order = [8, 7, 9, 6, 10, 5, 11, 4, 12, 3, 13, 2, 14, 1, 15]
    for i in order:
        to = zp(i)
        start(remote(outgoing.at[y, to], by_z.at[0, z], rz_s.at[0, to], rz_r.at[0, z], to * NY + y, head))
    by_z[0, z] = outgoing[y, z]
    for i in (1, 3, 2):
        remote(by_y.at[i], by_y.at[i], ry_s.at[i], ry_r.at[i], z * NY + yp(i), head).wait_recv()
    for i in order:
        to = zp(i)
        start(remote(
            by_y.at[1:, to], by_z.at[1:, z], rz_s.at[1, to], rz_r.at[1, z], to * NY + y, head
        ))
    by_z[1:, z] = by_y[1:, z]
    fresh_out = pltpu.make_async_copy(fresh, fresh_ref, out_s.at[4])
    fresh_out.start()

    their_weights(kw_ref).wait_send()
    for chunk in range(NZ):
        @pl.when(chunk // 2 != head)
        def _(chunk=chunk):
            remote(
                partial.at[chunk], received.at[x, c, 0],
                sum_s.at[chunk], sum_r.at[x, c, 0], seq, other,
            ).wait_send()
    clock[0] += 1000.0
    drain(0.0)
    outs = []
    for part in (0, 1):
        for i in reversed(order):
            frm = zp(i)
            region = by_z.at[0, frm] if part == 0 else by_z.at[1:, frm]
            remote(region, region, rz_s.at[part, frm], rz_r.at[part, frm], frm * NY + y, head).wait_recv()
        for r in range(NY):
            if (r == 0) == (part == 0):
                outs.append(pltpu.make_async_copy(by_z.at[r], routed_ref.at[:, yp(r)], out_s.at[r]))
                outs[-1].start()
    for copy in outs:
        copy.wait()
    fresh_out.wait()


def project(store_hidden, owner_row, new_hidden, key_columns, value_columns):
    dma = pltpu.SemaphoreType.DMA
    hbm = pl.BlockSpec(memory_space=pltpu.HBM)
    return pl.pallas_call(
        project_kernel,
        out_shape=(
            jax.ShapeDtypeStruct((NZ, NY, 2 * CAP, HD), jnp.bfloat16),
            jax.ShapeDtypeStruct((2, HD, TURN), jnp.float32),
        ),
        in_specs=[hbm] * 5,
        out_specs=(hbm, hbm),
        scratch_shapes=[
            pltpu.VMEM((ROWS, CHIP_FEAT), jnp.bfloat16),
            pltpu.VMEM((1, STORED), jnp.int32),
            pltpu.VMEM((NZ, NY, 16, CHIP_FEAT), jnp.bfloat16),
            pltpu.VMEM((NZ, NY, 16, ROWS), jnp.bfloat16),
            pltpu.VMEM((NX, 2, 2, NY, 16, ROWS), jnp.bfloat16),
            pltpu.VMEM((2 * NX, 8, ROWS), jnp.float32),
            pltpu.VMEM((HIST, STORED), jnp.bfloat16),
            pltpu.VMEM((HIST, HD), jnp.float32),
            pltpu.VMEM((2, HD, TURN), jnp.float32),
            pltpu.VMEM((NY, NZ, 2 * CAP, HD), jnp.bfloat16),
            pltpu.VMEM((NY, NZ, 2 * CAP, HD), jnp.bfloat16),
            pltpu.VMEM((NY, NZ, 2 * CAP, HD), jnp.bfloat16),
            dma((4,)), dma((5,)),
            dma((3,)), dma((3,)),
            dma((2, 17)), dma((2, 17)),
            dma((18, 2, 2)), dma((18, 2, 2)),
            dma((NZ,)), dma((NX, 2, 2)),
            dma((2 * NX,)), dma((2 * NX,)),
            dma((NY,)), dma((NY,)),
            dma((2, NZ)), dma((2, NZ)),
        ],
        compiler_params=pltpu.CompilerParams(
            collective_id=0, has_side_effects=True, vmem_limit_bytes=64 * 1024 * 1024
        ),
        name="project_rows",
    )(store_hidden, owner_row, new_hidden, key_columns, value_columns)


def attend_kernel(
    turn_ref, rows_ref, fresh_ref, query_ref, cos_ref, sin_ref, out_ref, key_ref, value_ref,
    rows_in, fresh_in, query_in, cos_in, sin_in, out, keys_out, values_out, in_s, out_s,
):
    def rotate(values, cosine, sine):
        return values * cosine + pltpu.roll(values, HD // 2, 1) * sine

    fetches = [
        pltpu.make_async_copy(src, dst, in_s.at[i])
        for i, (src, dst) in enumerate((
            (rows_ref, rows_in), (cos_ref, cos_in), (sin_ref, sin_in),
            (fresh_ref, fresh_in), (query_ref, query_in),
        ))
    ]
    for fetch in fetches:
        fetch.start()
    row_at = lax.broadcasted_iota(jnp.int32, (HIST, HIST), 0)
    lane_at = lax.broadcasted_iota(jnp.int32, (HIST, HIST), 1)
    before = jnp.where(lane_at < row_at, 1.0, 0.0).astype(jnp.bfloat16)
    fetches[0].wait()
    rows = rows_in[...].reshape(SESS, 2 * CAP, HD).astype(jnp.float32)
    sent_keys = rows[:, :CAP].reshape(HIST, HD)
    sent_values = rows[:, CAP:].reshape(HIST, HD)
    valid = jnp.abs(sent_keys) < EMPTY_TEST
    sent_keys = jnp.where(valid, sent_keys, 0.0).astype(jnp.bfloat16)
    marks = jnp.where(valid, 1.0, 0.0)
    position = jnp.dot(before, marks.astype(jnp.bfloat16), preferred_element_type=jnp.float32)
    position = jnp.where(valid, position, -1.0).T[:1].astype(jnp.int32)
    place = jnp.where(row_at == position, 1.0, 0.0).astype(jnp.bfloat16)
    history = jnp.dot(
        place,
        jnp.concatenate([sent_keys, sent_values.astype(jnp.bfloat16)], axis=1),
        preferred_element_type=jnp.float32,
    )
    length = jnp.sum(marks[:, :1]).astype(jnp.int32)
    turn = turn_ref[0]
    for fetch in fetches[1:]:
        fetch.wait()

    keys_out[0, :HIST] = rotate(history[:, :HD], cos_in[:HIST], sin_in[:HIST]).astype(jnp.bfloat16)
    values_out[0, :HIST] = history[:, HD:].astype(jnp.bfloat16)
    cosine = cos_in[pl.ds(length, TURN), :]
    sine = sin_in[pl.ds(length, TURN), :]
    live = lax.broadcasted_iota(jnp.int32, (TURN, HD), 0) < turn
    keys_out[0, HIST:] = jnp.where(live, rotate(fresh_in[0].T, cosine, sine), 0.0).astype(jnp.bfloat16)
    values_out[0, HIST:] = jnp.where(live, fresh_in[1].T, 0.0).astype(jnp.bfloat16)
    stores = [
        pltpu.make_async_copy(keys_out, key_ref, out_s.at[0]),
        pltpu.make_async_copy(values_out, value_ref, out_s.at[1]),
    ]
    for copy in stores:
        copy.start()

    keys = keys_out[0]
    values = values_out[0]
    slot_at = lax.broadcasted_iota(jnp.int32, (TURN, CACHE), 0)
    cache_at = lax.broadcasted_iota(jnp.int32, (TURN, CACHE), 1)
    allowed = (cache_at < length) | ((cache_at >= HIST) & (cache_at - HIST <= slot_at))
    for group in range(QH // KVH):
        at = pl.ds(group * HD, HD)
        query = rotate(query_in[:, at].astype(jnp.float32), cosine, sine).astype(jnp.bfloat16)
        scores = nt_dot(query, keys) * (1.0 / math.sqrt(HD))
        scores = jnp.where(allowed, scores, -jnp.inf)
        exponent = jnp.exp(scores - jnp.max(scores, axis=1, keepdims=True))
        weights = (exponent / jnp.sum(exponent, axis=1, keepdims=True)).astype(jnp.bfloat16)
        result = jnp.dot(weights, values, preferred_element_type=jnp.float32)
        out[group] = jnp.where(live, result, 0.0).astype(jnp.bfloat16)
        stores.append(pltpu.make_async_copy(out.at[group], out_ref.at[:, at], out_s.at[2 + group]))
        stores[-1].start()
    for copy in stores:
        copy.wait()


def attend(turn_length, rows, fresh, queries):
    cosine, sine = rotation_tables()
    hbm = pl.BlockSpec(memory_space=pltpu.HBM)
    groups = QH // KVH
    return pl.pallas_call(
        attend_kernel,
        out_shape=(
            jax.ShapeDtypeStruct((TURN, groups * HD), jnp.bfloat16),
            jax.ShapeDtypeStruct((1, CACHE, HD), jnp.bfloat16),
            jax.ShapeDtypeStruct((1, CACHE, HD), jnp.bfloat16),
        ),
        in_specs=[pl.BlockSpec(memory_space=pltpu.SMEM)] + [hbm] * 5,
        out_specs=(hbm, hbm, hbm),
        scratch_shapes=[
            pltpu.VMEM((NZ, NY, 2 * CAP, HD), jnp.bfloat16),
            pltpu.VMEM((2, HD, TURN), jnp.float32),
            pltpu.VMEM((TURN, groups * HD), jnp.bfloat16),
            pltpu.VMEM((CACHE, HD), jnp.float32),
            pltpu.VMEM((CACHE, HD), jnp.float32),
            pltpu.VMEM((groups, TURN, HD), jnp.bfloat16),
            pltpu.VMEM((1, CACHE, HD), jnp.bfloat16),
            pltpu.VMEM((1, CACHE, HD), jnp.bfloat16),
            pltpu.SemaphoreType.DMA((5,)),
            pltpu.SemaphoreType.DMA((2 + groups,)),
        ],
        compiler_params=pltpu.CompilerParams(vmem_limit_bytes=64 * 1024 * 1024),
        name="attend_turn",
    )(turn_length, rows, fresh, queries, jnp.asarray(cosine), jnp.asarray(sine))


def local(store_hidden, owner_map, new_hidden, new_lengths, queries, key_weight, value_weight):
    rows, fresh = project(
        store_hidden, owner_map.reshape(1, STORED), new_hidden, key_weight.T, value_weight.T
    )
    return attend(new_lengths, rows, fresh, queries)


def solution(mesh):
    placed = (
        P("seq", "head"),
        P("seq", None),
        P("seq", "head"),
        P("seq"),
        P("seq", "head"),
        P("head", "seq"),
        P("head", "seq"),
    )
    return jax.shard_map(
        local,
        mesh=mesh,
        in_specs=placed,
        out_specs=(P("seq", "head"), P("seq", None, "head"), P("seq", None, "head")),
        check_vma=False,
    )
```

```python
import functools
import math

import jax
import jax.numpy as jnp
import numpy as np
from jax import lax
from jax.experimental import pallas as pl
from jax.experimental.pallas import tpu as pltpu
from jax.sharding import PartitionSpec as P

D = 8192
QH = 64
KVH = 8
HD = 128
NZ = 16
NY = 4
NX = 4
STORED = 256
TURN = 128
ROWS = STORED + TURN
CAP = 8
SESS = NZ * NY
HIST = SESS * CAP
CACHE = HIST + TURN
FEAT = D // (2 * NX)
CHIP_FEAT = 2 * FEAT
SPLIT = 1536
WAYS = ((0, 1024), (1024, 2048), (1536, 2048))
OWN_WAYS = 2
EMPTY = float(2.0**100)
EMPTY_TEST = float(2.0**50)
MESH = pl.DeviceIdType.MESH
rope_base = 500000.0


def rotation_tables():
    half_index = np.arange(HD // 2, dtype=np.float64)
    inverse = 1.0 / np.power(rope_base, 2.0 * half_index / HD)
    wavelength = 2.0 * np.pi / inverse
    smooth = (8192.0 / wavelength - 1.0) / 3.0
    mixed = (1.0 - smooth) * inverse / 8.0 + smooth * inverse
    frequency = np.where(
        wavelength < 2048.0, inverse, np.where(wavelength > 8192.0, inverse / 8.0, mixed)
    )
    angles = np.arange(CACHE, dtype=np.float64)[:, None] * frequency[None, :]
    cosine, sine = np.cos(angles), np.sin(angles)
    return (
        np.concatenate([cosine, cosine], axis=1).astype(np.float32),
        np.concatenate([-sine, sine], axis=1).astype(np.float32),
    )


def nt_dot(a, b):
    return lax.dot_general(a, b, (((1,), (1,)), ((), ())), preferred_element_type=jnp.float32)


def project_kernel(
    store_ref, owner_ref, new_ref, kw_ref, vw_ref,
    routed_ref, fresh_ref,
    xs, owners, gathered, partial, received, squares, onehot, empties, fresh, outgoing, by_y,
    in_s, out_s, core_s, core_r, z_s, z_r, y_s, y_r, sum_s, sum_r, sq_s, sq_r, ry_s, ry_r, rz_s, rz_r,
):
    seq = lax.axis_index("seq")
    head = lax.axis_index("head")
    z, y = lax.div(seq, NY), lax.rem(seq, NY)
    x, c = lax.div(head, 2), lax.rem(head, 2)
    other = head + 1 - 2 * c

    def zp(delta):
        return lax.rem(z + delta + NZ, NZ)

    def yp(delta):
        return lax.rem(y + delta + NY, NY)

    def remote(src, dst, send_sem, recv_sem, to_seq, to_head):
        return pltpu.make_async_remote_copy(
            src_ref=src, dst_ref=dst, send_sem=send_sem, recv_sem=recv_sem,
            device_id=(to_seq, to_head), device_id_type=MESH,
        )

    clock = [0.0]
    sends = []

    def start(copy):
        copy.start()
        sends.append((clock[0], copy))

    def drain(age):
        while sends and sends[0][0] <= clock[0] - age:
            sends.pop(0)[1].wait_send()

    barrier = pltpu.get_barrier_semaphore()
    peers = [(z * NY + yp(i), head) for i in (1, -1)]
    peers += [(zp(i) * NY + y, head) for i in (1, -1)]
    peers += [(seq, lax.rem(head + i, 2 * NX)) for i in range(1, 2 * NX)]
    for peer in peers:
        pl.semaphore_signal(barrier, inc=1, device_id=peer, device_id_type=MESH)

    own = pl.ds(pl.multiple_of(c * FEAT, FEAT), FEAT)
    theirs = pl.ds(pl.multiple_of((1 - c) * FEAT, FEAT), FEAT)
    mine = gathered.at[0, 0, :, own]

    def own_weights(ref):
        return pltpu.make_async_copy(ref, mine, in_s.at[0])

    def their_weights(ref):
        return remote(ref, mine, core_s.at[0], core_r.at[0], seq, other)

    @pl.when(c == 0)
    def _():
        own_weights(kw_ref).start()

    @pl.when(c == 1)
    def _():
        own_weights(vw_ref).start()

    store_in = pltpu.make_async_copy(store_ref, xs.at[:STORED, own], in_s.at[1])
    new_in = pltpu.make_async_copy(new_ref, xs.at[STORED:, own], in_s.at[2])
    owner_in = pltpu.make_async_copy(owner_ref, owners, in_s.at[3])
    for copy in (store_in, new_in, owner_in):
        copy.start()
    pl.semaphore_wait(barrier, len(peers))

    @pl.when(c == 0)
    def _():
        their_weights(vw_ref).start()

    @pl.when(c == 1)
    def _():
        their_weights(kw_ref).start()

    own_weights(kw_ref).wait()
    remote(
        kw_ref, gathered.at[0, 0, :, theirs], core_s.at[0], core_r.at[0], seq, other
    ).wait_recv()

    far = NZ // 2

    def slot_of(m):
        if abs(m) == far:
            return NZ - 1
        return 2 * m - 1 if m > 0 else -2 * m

    def z_region(way, m):
        lo, hi = WAYS[way]
        if way < OWN_WAYS:
            return gathered.at[slot_of(m), 0, :, lo:hi]
        return gathered.at[slot_of(m), 1:, :, lo:hi]

    def z_send(way, m, step):
        at = m + step + far
        start(remote(
            z_region(way, m), z_region(way, m + step),
            z_s.at[way, at], z_r.at[way, at], zp(step) * NY + y, head,
        ))

    def z_take(way, m):
        region = z_region(way, m)
        remote(region, region, z_s.at[way, m + far], z_r.at[way, m + far], seq, head).wait_recv()

    def onward(way, m):
        if m == 0:
            return [1, -1]
        sign = 1 if m > 0 else -1
        last = far if (sign == 1) == (way % 2 == 0) else far - 1
        return [sign] if abs(m) < last else []

    def z_first(way):
        for step in onward(way, 0):
            z_send(way, 0, step)

    def z_pass(way, t):
        for m in (t, -t):
            if onward(way, m - (1 if m > 0 else -1)):
                z_take(way, m)
                for step in onward(way, m):
                    z_send(way, m, step)

    def chunks_of(t):
        return slice(slot_of(t), slot_of(t) + (1 if t in (0, far) else 2))

    def half_way(lo, hi):
        return lo + (hi - lo) // 256 * 128

    def y_piece(index, stage, d, src, dst):
        return remote(
            src, dst, y_s.at[index, stage, d], y_r.at[index, stage, d],
            z * NY + yp(1 if d == 0 else -1), head,
        )

    def y_one(index, t, lo, hi):
        at = chunks_of(t)
        for d in (0, 1):
            start(y_piece(
                index, 0, d, gathered.at[at, 0, :, lo:hi], gathered.at[at, 3 - 2 * d, :, lo:hi]
            ))

    def y_two(index, t, lo, hi):
        at = chunks_of(t)
        mid = half_way(lo, hi)
        for d in (0, 1):
            whole = gathered.at[at, 3 - 2 * d, :, lo:hi]
            y_piece(index, 0, d, whole, whole).wait_recv()
            part = slice(lo, mid) if d == 0 else slice(mid, hi)
            start(y_piece(
                index, 1, d, gathered.at[at, 3 - 2 * d, :, part], gathered.at[at, 2, :, part]
            ))

    def y_end(index, t, lo, hi):
        at = chunks_of(t)
        mid = half_way(lo, hi)
        for d in (0, 1):
            region = gathered.at[at, 2, :, lo:mid] if d == 0 else gathered.at[at, 2, :, mid:hi]
            y_piece(index, 1, d, region, region).wait_recv()

    def sum_squares():
        store_in.wait()
        new_in.wait()
        ones = jnp.ones((8, 256), jnp.bfloat16)
        total = jnp.zeros((8, ROWS), jnp.float32)
        for piece in range(FEAT // 256):
            at = pl.ds(pl.multiple_of(c * FEAT + piece * 256, 256), 256)
            block = xs[:, at].astype(jnp.float32)
            square = block * block
            high = square.astype(jnp.bfloat16)
            low = (square - high.astype(jnp.float32)).astype(jnp.bfloat16)
            total += nt_dot(ones, high) + nt_dot(ones, low)
        squares[head] = total
        for i in range(1, 2 * NX):
            to = lax.rem(head + i, 2 * NX)
            start(remote(squares.at[head], squares.at[head], sq_s.at[to], sq_r.at[head], seq, to))

    def find_slots():
        owner_in.wait()
        owner_row = owners[...]
        owner_lanes = jnp.broadcast_to(owner_row.astype(jnp.float32), (STORED, STORED))
        earlier = lax.broadcasted_iota(jnp.int32, (STORED, STORED), 0) < lax.broadcasted_iota(
            jnp.int32, (STORED, STORED), 1
        )
        same = jnp.where(earlier & (owner_lanes.T == owner_lanes), 1.0, 0.0)
        rank = jnp.sum(same, axis=0, keepdims=True).astype(jnp.int32)
        owner_z = lax.shift_right_logical(owner_row, 2)
        owner_y = lax.bitwise_and(owner_row, 3)
        slot = (owner_y * NZ + owner_z) * CAP + rank
        hot = jnp.where(lax.broadcasted_iota(jnp.int32, (HIST, STORED), 0) == slot, 1.0, 0.0)
        onehot[...] = hot.astype(jnp.bfloat16)
        filled = jnp.sum(hot, axis=1, keepdims=True)
        empties[...] = jnp.broadcast_to((1.0 - filled) * EMPTY, (HIST, HD))

    def send_rows():
        start(remote(store_ref, xs.at[:STORED, own], core_s.at[1], core_r.at[1], seq, other))
        start(remote(new_ref, xs.at[STORED:, own], core_s.at[2], core_r.at[2], seq, other))

    def take_rows():
        for i, rows in ((1, slice(0, STORED)), (2, slice(STORED, ROWS))):
            region = xs.at[rows, theirs]
            remote(region, region, core_s.at[i], core_r.at[i], seq, other).wait_recv()

    def sum_send(m):
        slot = slot_of(m)
        chunk = zp(-m)
        to = lax.div(chunk, 2)
        half = lax.rem(chunk, 2)
        return slot, half, to, remote(
            partial.at[slot], received.at[x, c, half],
            sum_s.at[slot], sum_r.at[x, c, half], seq, to,
        )

    def send_sums(t):
        at = chunks_of(t)
        count = at.stop - at.start
        result = nt_dot(gathered[at].reshape(count * 64, CHIP_FEAT), xs[...]).astype(jnp.bfloat16)
        for i in range(count):
            m = t if i == 0 else -t
            slot, half, to, copy = sum_send(m)
            for r in range(NY):
                row = i * 64 + r * 16
                partial[slot, yp(r)] = result[row : row + 16]

            @pl.when(to == head)
            def _(slot=slot, half=half):
                received[x, c, half] = partial[slot]

            @pl.when(to != head)
            def _(copy=copy):
                copy.start()

    z_first(0)
    y_one(9, 0, SPLIT, CHIP_FEAT)
    sum_squares()
    z_first(1)
    y_one(0, 0, 0, SPLIT)
    send_rows()
    for s in range(1, far + 3):
        clock[0] = 2.6 * s
        if s <= far:
            z_pass(0, s)
            if s == 1:
                y_two(9, 0, SPLIT, CHIP_FEAT)
            z_pass(1, s)
            y_one(s, s, 0, SPLIT)
        if s == 2:
            y_end(9, 0, SPLIT, CHIP_FEAT)
            for way in range(OWN_WAYS, len(WAYS)):
                z_first(way)
            find_slots()
            take_rows()
        elif 1 <= s - 2 <= far:
            for way in range(OWN_WAYS, len(WAYS)):
                z_pass(way, s - 2)
        if s - 1 <= far:
            y_two(s - 1, s - 1, 0, SPLIT)
        if s >= 2:
            y_end(s - 2, s - 2, 0, SPLIT)
            send_sums(s - 2)
        drain(6.0)

    for i in range(1, 2 * NX):
        frm = lax.rem(head + i, 2 * NX)
        remote(squares.at[frm], squares.at[frm], sq_s.at[frm], sq_r.at[frm], seq, frm).wait_recv()
    sums = jnp.sum(jnp.sum(squares[...], axis=0), axis=0, keepdims=True) * 0.125
    scale = lax.rsqrt(sums / D + 1e-05)
    for i in range(1, 2 * NX):
        frm = lax.rem(head + i, 2 * NX)
        fx, fc = lax.div(frm, 2), lax.rem(frm, 2)
        for half in (0, 1):
            remote(
                received.at[fx, fc, half], received.at[fx, fc, half],
                sum_s.at[0], sum_r.at[fx, fc, half], seq, frm,
            ).wait_recv()
    kinds = []
    for kind in (0, 1):
        summed = jnp.zeros((HD, ROWS), jnp.float32)
        for fx in range(NX):
            summed += received[fx, kind].reshape(HD, ROWS).astype(jnp.float32)
        scaled = summed * scale
        fresh[kind] = scaled[:, STORED:]
        kinds.append(nt_dot(onehot[...], scaled[:, :STORED].astype(jnp.bfloat16)))
    keys = kinds[0] + empties[...]
    slots = jnp.concatenate(
        [keys.reshape(SESS, CAP, HD), kinds[1].reshape(SESS, CAP, HD)], axis=1
    )
    outgoing[...] = slots.astype(jnp.bfloat16).reshape(NY, NZ, 2 * CAP, HD)

    for i in (2, 1, 3):
        to = yp(i)
        start(remote(outgoing.at[to], by_y.at[NY - i], ry_s.at[i], ry_r.at[NY - i], z * NY + to, head))
    order = [8, 7, 9, 6, 10, 5, 11, 4, 12, 3, 13, 2, 14, 1, 15]
    for i in order:
        to = zp(i)
        start(remote(
            outgoing.at[y, to], routed_ref.at[0, z], rz_s.at[0, to], rz_r.at[0, z], to * NY + y, head
        ))
    for i in (1, 3, 2):
        remote(by_y.at[i], by_y.at[i], ry_s.at[i], ry_r.at[i], z * NY + yp(i), head).wait_recv()
    for i in order:
        to = zp(i)
        start(remote(
            by_y.at[1:, to], routed_ref.at[1:, z], rz_s.at[1, to], rz_r.at[1, z], to * NY + y, head
        ))
    outs = [
        pltpu.make_async_copy(outgoing.at[y, z], routed_ref.at[0, z], out_s.at[0]),
        pltpu.make_async_copy(by_y.at[1:, z], routed_ref.at[1:, z], out_s.at[1]),
    ]
    for copy in outs:
        copy.start()
    fresh_out = pltpu.make_async_copy(fresh, fresh_ref, out_s.at[4])
    fresh_out.start()

    their_weights(kw_ref).wait_send()
    for m in range(1 - far, far + 1):
        _, _, to, copy = sum_send(m)
        pl.when(to != head)(copy.wait_send)
    clock[0] += 1000.0
    drain(0.0)
    for part in (0, 1):
        for i in reversed(order):
            frm = zp(i)
            region = routed_ref.at[0, frm] if part == 0 else routed_ref.at[1:, frm]
            remote(region, region, rz_s.at[part, frm], rz_r.at[part, frm], frm * NY + y, head).wait_recv()
    for copy in outs:
        copy.wait()
    fresh_out.wait()


def project(store_hidden, owner_row, new_hidden, key_columns, value_columns):
    dma = pltpu.SemaphoreType.DMA
    hbm = pl.BlockSpec(memory_space=pltpu.HBM)
    return pl.pallas_call(
        project_kernel,
        out_shape=(
            jax.ShapeDtypeStruct((NY, NZ, 2 * CAP, HD), jnp.bfloat16),
            jax.ShapeDtypeStruct((2, HD, TURN), jnp.float32),
        ),
        in_specs=[hbm] * 5,
        out_specs=(hbm, hbm),
        scratch_shapes=[
            pltpu.VMEM((ROWS, CHIP_FEAT), jnp.bfloat16),
            pltpu.VMEM((1, STORED), jnp.int32),
            pltpu.VMEM((NZ, NY, 16, CHIP_FEAT), jnp.bfloat16),
            pltpu.VMEM((NZ, NY, 16, ROWS), jnp.bfloat16),
            pltpu.VMEM((NX, 2, 2, NY, 16, ROWS), jnp.bfloat16),
            pltpu.VMEM((2 * NX, 8, ROWS), jnp.float32),
            pltpu.VMEM((HIST, STORED), jnp.bfloat16),
            pltpu.VMEM((HIST, HD), jnp.float32),
            pltpu.VMEM((2, HD, TURN), jnp.float32),
            pltpu.VMEM((NY, NZ, 2 * CAP, HD), jnp.bfloat16),
            pltpu.VMEM((NY, NZ, 2 * CAP, HD), jnp.bfloat16),
            dma((4,)), dma((5,)),
            dma((3,)), dma((3,)),
            dma((len(WAYS), NZ + 1)), dma((len(WAYS), NZ + 1)),
            dma((10, 2, 2)), dma((10, 2, 2)),
            dma((NZ,)), dma((NX, 2, 2)),
            dma((2 * NX,)), dma((2 * NX,)),
            dma((NY,)), dma((NY,)),
            dma((2, NZ)), dma((2, NZ)),
        ],
        compiler_params=pltpu.CompilerParams(
            collective_id=0, has_side_effects=True, vmem_limit_bytes=64 * 1024 * 1024
        ),
        name="project_rows",
    )(store_hidden, owner_row, new_hidden, key_columns, value_columns)


def attend_kernel(
    turn_ref, rows_ref, fresh_ref, query_ref, cos_ref, sin_ref, out_ref, key_ref, value_ref,
    rows_in, fresh_in, query_in, cos_in, sin_in, out, keys_out, values_out, in_s, out_s,
):
    def rotate(values, cosine, sine):
        return values * cosine + pltpu.roll(values, HD // 2, 1) * sine

    y = lax.rem(lax.axis_index("seq"), NY)
    fetches = [
        pltpu.make_async_copy(src, dst, in_s.at[i])
        for i, (src, dst) in enumerate(
            [(rows_ref.at[r], rows_in.at[:, lax.rem(y + r, NY)]) for r in range(NY)]
            + [(cos_ref, cos_in), (sin_ref, sin_in), (fresh_ref, fresh_in), (query_ref, query_in)]
        )
    ]
    for fetch in fetches:
        fetch.start()
    row_at = lax.broadcasted_iota(jnp.int32, (HIST, HIST), 0)
    lane_at = lax.broadcasted_iota(jnp.int32, (HIST, HIST), 1)
    before = jnp.where(lane_at < row_at, 1.0, 0.0).astype(jnp.bfloat16)
    for fetch in fetches[:NY]:
        fetch.wait()
    rows = rows_in[...].reshape(SESS, 2 * CAP, HD).astype(jnp.float32)
    sent_keys = rows[:, :CAP].reshape(HIST, HD)
    sent_values = rows[:, CAP:].reshape(HIST, HD)
    valid = jnp.abs(sent_keys) < EMPTY_TEST
    sent_keys = jnp.where(valid, sent_keys, 0.0).astype(jnp.bfloat16)
    marks = jnp.where(valid, 1.0, 0.0)
    position = jnp.dot(before, marks.astype(jnp.bfloat16), preferred_element_type=jnp.float32)
    position = jnp.where(valid, position, -1.0).T[:1].astype(jnp.int32)
    place = jnp.where(row_at == position, 1.0, 0.0).astype(jnp.bfloat16)
    history = jnp.dot(
        place,
        jnp.concatenate([sent_keys, sent_values.astype(jnp.bfloat16)], axis=1),
        preferred_element_type=jnp.float32,
    )
    length = jnp.sum(marks[:, :1]).astype(jnp.int32)
    turn = turn_ref[0]
    for fetch in fetches[NY:]:
        fetch.wait()

    keys_out[0, :HIST] = rotate(history[:, :HD], cos_in[:HIST], sin_in[:HIST]).astype(jnp.bfloat16)
    values_out[0, :HIST] = history[:, HD:].astype(jnp.bfloat16)
    cosine = cos_in[pl.ds(length, TURN), :]
    sine = sin_in[pl.ds(length, TURN), :]
    live = lax.broadcasted_iota(jnp.int32, (TURN, HD), 0) < turn
    keys_out[0, HIST:] = jnp.where(live, rotate(fresh_in[0].T, cosine, sine), 0.0).astype(jnp.bfloat16)
    values_out[0, HIST:] = jnp.where(live, fresh_in[1].T, 0.0).astype(jnp.bfloat16)
    stores = [
        pltpu.make_async_copy(keys_out, key_ref, out_s.at[0]),
        pltpu.make_async_copy(values_out, value_ref, out_s.at[1]),
    ]
    for copy in stores:
        copy.start()

    keys = keys_out[0]
    values = values_out[0]
    slot_at = lax.broadcasted_iota(jnp.int32, (TURN, CACHE), 0)
    cache_at = lax.broadcasted_iota(jnp.int32, (TURN, CACHE), 1)
    allowed = (cache_at < length) | ((cache_at >= HIST) & (cache_at - HIST <= slot_at))
    for group in range(QH // KVH):
        at = pl.ds(group * HD, HD)
        query = rotate(query_in[:, at].astype(jnp.float32), cosine, sine).astype(jnp.bfloat16)
        scores = jnp.where(allowed, nt_dot(query, keys), -jnp.inf)
        highest = jnp.max(scores, axis=1, keepdims=True)
        exponent = jnp.exp2((scores - highest) * (math.log2(math.e) / math.sqrt(HD)))
        total = jnp.sum(exponent, axis=1, keepdims=True)
        result = jnp.dot(exponent.astype(jnp.bfloat16), values, preferred_element_type=jnp.float32)
        result = result * (1.0 / total)
        out[group] = jnp.where(live, result, 0.0).astype(jnp.bfloat16)
        stores.append(pltpu.make_async_copy(out.at[group], out_ref.at[:, at], out_s.at[2 + group]))
        stores[-1].start()
    for copy in stores:
        copy.wait()


def attend(turn_length, rows, fresh, queries):
    cosine, sine = rotation_tables()
    hbm = pl.BlockSpec(memory_space=pltpu.HBM)
    groups = QH // KVH
    return pl.pallas_call(
        attend_kernel,
        out_shape=(
            jax.ShapeDtypeStruct((TURN, groups * HD), jnp.bfloat16),
            jax.ShapeDtypeStruct((1, CACHE, HD), jnp.bfloat16),
            jax.ShapeDtypeStruct((1, CACHE, HD), jnp.bfloat16),
        ),
        in_specs=[pl.BlockSpec(memory_space=pltpu.SMEM)] + [hbm] * 5,
        out_specs=(hbm, hbm, hbm),
        scratch_shapes=[
            pltpu.VMEM((NZ, NY, 2 * CAP, HD), jnp.bfloat16),
            pltpu.VMEM((2, HD, TURN), jnp.float32),
            pltpu.VMEM((TURN, groups * HD), jnp.bfloat16),
            pltpu.VMEM((CACHE, HD), jnp.float32),
            pltpu.VMEM((CACHE, HD), jnp.float32),
            pltpu.VMEM((groups, TURN, HD), jnp.bfloat16),
            pltpu.VMEM((1, CACHE, HD), jnp.bfloat16),
            pltpu.VMEM((1, CACHE, HD), jnp.bfloat16),
            pltpu.SemaphoreType.DMA((4 + NY,)),
            pltpu.SemaphoreType.DMA((2 + groups,)),
        ],
        compiler_params=pltpu.CompilerParams(vmem_limit_bytes=64 * 1024 * 1024),
        name="attend_turn",
    )(turn_length, rows, fresh, queries, jnp.asarray(cosine), jnp.asarray(sine))


def local(store_hidden, owner_map, new_hidden, new_lengths, queries, key_weight, value_weight):
    rows, fresh = project(
        store_hidden, owner_map.reshape(1, STORED), new_hidden, key_weight.T, value_weight.T
    )
    return attend(new_lengths, rows, fresh, queries)


def solution(mesh):
    placed = (
        P("seq", "head"),
        P("seq", None),
        P("seq", "head"),
        P("seq"),
        P("seq", "head"),
        P("head", "seq"),
        P("head", "seq"),
    )
    return jax.shard_map(
        local,
        mesh=mesh,
        in_specs=placed,
        out_specs=(P("seq", "head"), P("seq", None, "head"), P("seq", None, "head")),
        check_vma=False,
    )
```

```python
import functools
import math

import jax
import jax.numpy as jnp
import numpy as np
from jax import lax
from jax.experimental import pallas as pl
from jax.experimental.pallas import tpu as pltpu
from jax.sharding import PartitionSpec as P

D = 8192
QH = 64
KVH = 8
HD = 128
NZ = 16
NY = 4
NX = 4
STORED = 256
TURN = 128
ROWS = STORED + TURN
CAP = 8
SESS = NZ * NY
HIST = SESS * CAP
CACHE = HIST + TURN
FEAT = D // (2 * NX)
CHIP_FEAT = 2 * FEAT
SPLIT = 1536
WAYS = ((0, 1024), (1024, 2048), (1536, 2048))
OWN_WAYS = 2
EMPTY = float(2.0**100)
EMPTY_TEST = float(2.0**50)
MESH = pl.DeviceIdType.MESH
rope_base = 500000.0


def rotation_tables():
    half_index = np.arange(HD // 2, dtype=np.float64)
    inverse = 1.0 / np.power(rope_base, 2.0 * half_index / HD)
    wavelength = 2.0 * np.pi / inverse
    smooth = (8192.0 / wavelength - 1.0) / 3.0
    mixed = (1.0 - smooth) * inverse / 8.0 + smooth * inverse
    frequency = np.where(
        wavelength < 2048.0, inverse, np.where(wavelength > 8192.0, inverse / 8.0, mixed)
    )
    angles = np.arange(CACHE, dtype=np.float64)[:, None] * frequency[None, :]
    cosine, sine = np.cos(angles), np.sin(angles)
    return (
        np.concatenate([cosine, cosine], axis=1).astype(np.float32),
        np.concatenate([-sine, sine], axis=1).astype(np.float32),
    )


def nt_dot(a, b):
    return lax.dot_general(a, b, (((1,), (1,)), ((), ())), preferred_element_type=jnp.float32)


def project_kernel(
    store_ref, owner_ref, new_ref, kw_ref, vw_ref,
    routed_ref, fresh_ref,
    xs, owners, gathered, partial, received, squares, onehot, empties, fresh, outgoing, by_y,
    in_s, out_s, core_s, core_r, z_s, z_r, y_s, y_r, sum_s, sum_r, sq_s, sq_r, ry_s, ry_r, rz_s, rz_r,
):
    seq = lax.axis_index("seq")
    head = lax.axis_index("head")
    z, y = lax.div(seq, NY), lax.rem(seq, NY)
    x, c = lax.div(head, 2), lax.rem(head, 2)
    other = head + 1 - 2 * c

    def zp(delta):
        return lax.rem(z + delta + NZ, NZ)

    def yp(delta):
        return lax.rem(y + delta + NY, NY)

    def remote(src, dst, send_sem, recv_sem, to_seq, to_head):
        return pltpu.make_async_remote_copy(
            src_ref=src, dst_ref=dst, send_sem=send_sem, recv_sem=recv_sem,
            device_id=(to_seq, to_head), device_id_type=MESH,
        )

    clock = [0.0]
    sends = []

    def start(copy):
        copy.start()
        sends.append((clock[0], copy))

    def drain(age):
        while sends and sends[0][0] <= clock[0] - age:
            sends.pop(0)[1].wait_send()

    barrier = pltpu.get_barrier_semaphore()
    peers = [(z * NY + yp(i), head) for i in (1, -1)]
    peers += [(zp(i) * NY + y, head) for i in (1, -1)]
    peers += [(seq, lax.rem(head + i, 2 * NX)) for i in range(1, 2 * NX)]
    for peer in peers:
        pl.semaphore_signal(barrier, inc=1, device_id=peer, device_id_type=MESH)

    own = pl.ds(pl.multiple_of(c * FEAT, FEAT), FEAT)
    theirs = pl.ds(pl.multiple_of((1 - c) * FEAT, FEAT), FEAT)
    mine = gathered.at[0, 0, :, own]

    def own_weights(ref):
        return pltpu.make_async_copy(ref, mine, in_s.at[0])

    def their_weights(ref):
        return remote(ref, mine, core_s.at[0], core_r.at[0], seq, other)

    @pl.when(c == 0)
    def _():
        own_weights(kw_ref).start()

    @pl.when(c == 1)
    def _():
        own_weights(vw_ref).start()

    store_in = pltpu.make_async_copy(store_ref, xs.at[:STORED, own], in_s.at[1])
    new_in = pltpu.make_async_copy(new_ref, xs.at[STORED:, own], in_s.at[2])
    owner_in = pltpu.make_async_copy(owner_ref, owners, in_s.at[3])
    for copy in (store_in, new_in, owner_in):
        copy.start()
    pl.semaphore_wait(barrier, len(peers))

    @pl.when(c == 0)
    def _():
        their_weights(vw_ref).start()

    @pl.when(c == 1)
    def _():
        their_weights(kw_ref).start()

    own_weights(kw_ref).wait()
    remote(
        kw_ref, gathered.at[0, 0, :, theirs], core_s.at[0], core_r.at[0], seq, other
    ).wait_recv()

    far = NZ // 2

    def slot_of(m):
        if abs(m) == far:
            return NZ - 1
        return 2 * m - 1 if m > 0 else -2 * m

    def z_region(way, m):
        lo, hi = WAYS[way]
        if way < OWN_WAYS:
            return gathered.at[slot_of(m), 0, :, lo:hi]
        return gathered.at[slot_of(m), 1:, :, lo:hi]

    def z_send(way, m, step):
        at = m + step + far
        start(remote(
            z_region(way, m), z_region(way, m + step),
            z_s.at[way, at], z_r.at[way, at], zp(step) * NY + y, head,
        ))

    def z_take(way, m):
        region = z_region(way, m)
        remote(region, region, z_s.at[way, m + far], z_r.at[way, m + far], seq, head).wait_recv()

    def onward(way, m):
        if m == 0:
            return [1, -1]
        sign = 1 if m > 0 else -1
        last = far if (sign == 1) == (way % 2 == 0) else far - 1
        return [sign] if abs(m) < last else []

    def z_first(way):
        for step in onward(way, 0):
            z_send(way, 0, step)

    def z_pass(way, t):
        for m in (t, -t):
            if onward(way, m - (1 if m > 0 else -1)):
                z_take(way, m)
                for step in onward(way, m):
                    z_send(way, m, step)

    def chunks_of(t):
        return slice(slot_of(t), slot_of(t) + (1 if t in (0, far) else 2))

    def half_way(lo, hi):
        return lo + (hi - lo) // 256 * 128

    def y_piece(index, stage, d, src, dst):
        return remote(
            src, dst, y_s.at[index, stage, d], y_r.at[index, stage, d],
            z * NY + yp(1 if d == 0 else -1), head,
        )

    def y_one(index, t, lo, hi):
        at = chunks_of(t)
        for d in (0, 1):
            start(y_piece(
                index, 0, d, gathered.at[at, 0, :, lo:hi], gathered.at[at, 3 - 2 * d, :, lo:hi]
            ))

    def y_two(index, t, lo, hi):
        at = chunks_of(t)
        mid = half_way(lo, hi)
        for d in (0, 1):
            whole = gathered.at[at, 3 - 2 * d, :, lo:hi]
            y_piece(index, 0, d, whole, whole).wait_recv()
            part = slice(lo, mid) if d == 0 else slice(mid, hi)
            start(y_piece(
                index, 1, d, gathered.at[at, 3 - 2 * d, :, part], gathered.at[at, 2, :, part]
            ))

    def y_end(index, t, lo, hi):
        at = chunks_of(t)
        mid = half_way(lo, hi)
        for d in (0, 1):
            region = gathered.at[at, 2, :, lo:mid] if d == 0 else gathered.at[at, 2, :, mid:hi]
            y_piece(index, 1, d, region, region).wait_recv()

    def sum_squares():
        store_in.wait()
        new_in.wait()
        ones = jnp.ones((8, 256), jnp.bfloat16)
        total = jnp.zeros((8, ROWS), jnp.float32)
        for piece in range(FEAT // 256):
            at = pl.ds(pl.multiple_of(c * FEAT + piece * 256, 256), 256)
            block = xs[:, at].astype(jnp.float32)
            square = block * block
            high = square.astype(jnp.bfloat16)
            low = (square - high.astype(jnp.float32)).astype(jnp.bfloat16)
            total += nt_dot(ones, high) + nt_dot(ones, low)
        squares[head] = total
        for i in range(1, 2 * NX):
            to = lax.rem(head + i, 2 * NX)
            start(remote(squares.at[head], squares.at[head], sq_s.at[to], sq_r.at[head], seq, to))

    def find_slots():
        owner_in.wait()
        owner_row = owners[...]
        owner_lanes = jnp.broadcast_to(owner_row.astype(jnp.float32), (STORED, STORED))
        earlier = lax.broadcasted_iota(jnp.int32, (STORED, STORED), 0) < lax.broadcasted_iota(
            jnp.int32, (STORED, STORED), 1
        )
        same = jnp.where(earlier & (owner_lanes.T == owner_lanes), 1.0, 0.0)
        rank = jnp.sum(same, axis=0, keepdims=True).astype(jnp.int32)
        owner_z = lax.shift_right_logical(owner_row, 2)
        owner_y = lax.bitwise_and(owner_row, 3)
        slot = (owner_y * NZ + owner_z) * CAP + rank
        hot = jnp.where(lax.broadcasted_iota(jnp.int32, (HIST, STORED), 0) == slot, 1.0, 0.0)
        onehot[...] = hot.astype(jnp.bfloat16)
        filled = jnp.sum(hot, axis=1, keepdims=True)
        empties[...] = jnp.broadcast_to((1.0 - filled) * EMPTY, (HIST, HD))

    def send_rows():
        start(remote(store_ref, xs.at[:STORED, own], core_s.at[1], core_r.at[1], seq, other))
        start(remote(new_ref, xs.at[STORED:, own], core_s.at[2], core_r.at[2], seq, other))

    def take_rows():
        for i, rows in ((1, slice(0, STORED)), (2, slice(STORED, ROWS))):
            region = xs.at[rows, theirs]
            remote(region, region, core_s.at[i], core_r.at[i], seq, other).wait_recv()

    def sum_send(m):
        slot = slot_of(m)
        chunk = zp(-m)
        to = lax.div(chunk, 2)
        half = lax.rem(chunk, 2)
        return slot, half, to, remote(
            partial.at[slot], received.at[x, c, half],
            sum_s.at[slot], sum_r.at[x, c, half], seq, to,
        )

    def send_sums(t):
        at = chunks_of(t)
        count = at.stop - at.start
        result = nt_dot(gathered[at].reshape(count * 64, CHIP_FEAT), xs[...]).astype(jnp.bfloat16)
        for i in range(count):
            m = t if i == 0 else -t
            slot, half, to, copy = sum_send(m)
            for r in range(NY):
                row = i * 64 + r * 16
                partial[slot, yp(r)] = result[row : row + 16]

            @pl.when(to == head)
            def _(slot=slot, half=half):
                received[x, c, half] = partial[slot]

            @pl.when(to != head)
            def _(copy=copy):
                copy.start()

    z_first(0)
    y_one(9, 0, SPLIT, CHIP_FEAT)
    sum_squares()
    z_first(1)
    y_one(0, 0, 0, SPLIT)
    send_rows()
    for s in range(1, far + 3):
        clock[0] = 2.6 * s
        if s <= far:
            z_pass(0, s)
            if s == 1:
                y_two(9, 0, SPLIT, CHIP_FEAT)
            z_pass(1, s)
            y_one(s, s, 0, SPLIT)
        if s == 2:
            y_end(9, 0, SPLIT, CHIP_FEAT)
            for way in range(OWN_WAYS, len(WAYS)):
                z_first(way)
            find_slots()
            take_rows()
        elif 1 <= s - 2 <= far:
            for way in range(OWN_WAYS, len(WAYS)):
                z_pass(way, s - 2)
        if s - 1 <= far:
            y_two(s - 1, s - 1, 0, SPLIT)
        if s >= 2:
            y_end(s - 2, s - 2, 0, SPLIT)
            send_sums(s - 2)
        drain(6.0)

    for i in range(1, 2 * NX):
        frm = lax.rem(head + i, 2 * NX)
        remote(squares.at[frm], squares.at[frm], sq_s.at[frm], sq_r.at[frm], seq, frm).wait_recv()
    sums = jnp.sum(jnp.sum(squares[...], axis=0), axis=0, keepdims=True) * 0.125
    scale = lax.rsqrt(sums / D + 1e-05)
    for i in range(1, 2 * NX):
        frm = lax.rem(head + i, 2 * NX)
        fx, fc = lax.div(frm, 2), lax.rem(frm, 2)
        for half in (0, 1):
            remote(
                received.at[fx, fc, half], received.at[fx, fc, half],
                sum_s.at[0], sum_r.at[fx, fc, half], seq, frm,
            ).wait_recv()
    kinds = []
    for kind in (0, 1):
        summed = jnp.zeros((HD, ROWS), jnp.float32)
        for fx in range(NX):
            summed += received[fx, kind].reshape(HD, ROWS).astype(jnp.float32)
        scaled = summed * scale
        fresh[kind] = scaled[:, STORED:]
        kinds.append(nt_dot(onehot[...], scaled[:, :STORED].astype(jnp.bfloat16)))
    keys = kinds[0] + empties[...]
    slots = jnp.concatenate(
        [keys.reshape(SESS, CAP, HD), kinds[1].reshape(SESS, CAP, HD)], axis=1
    )
    outgoing[...] = slots.astype(jnp.bfloat16).reshape(NY, NZ, 2 * CAP, HD)

    for i in (2, 1, 3):
        to = yp(i)
        start(remote(outgoing.at[to], by_y.at[NY - i], ry_s.at[i], ry_r.at[NY - i], z * NY + to, head))
    order = [8, 7, 9, 6, 10, 5, 11, 4, 12, 3, 13, 2, 14, 1, 15]
    for i in order:
        to = zp(i)
        start(remote(
            outgoing.at[y, to], routed_ref.at[0, z], rz_s.at[0, to], rz_r.at[0, z], to * NY + y, head
        ))
    for i in (1, 3, 2):
        remote(by_y.at[i], by_y.at[i], ry_s.at[i], ry_r.at[i], z * NY + yp(i), head).wait_recv()
    for group in (order[:3], order[3:7], order[7:]):
        copies = []
        for i in group:
            to = zp(i)
            copies.append(remote(
                by_y.at[1:, to], routed_ref.at[1:, z], rz_s.at[1, to], rz_r.at[1, z], to * NY + y, head
            ))
            copies[-1].start()
        for copy in copies:
            copy.wait_send()
    outs = [
        pltpu.make_async_copy(outgoing.at[y, z], routed_ref.at[0, z], out_s.at[0]),
        pltpu.make_async_copy(by_y.at[1:, z], routed_ref.at[1:, z], out_s.at[1]),
    ]
    for copy in outs:
        copy.start()
    fresh_out = pltpu.make_async_copy(fresh, fresh_ref, out_s.at[4])
    fresh_out.start()

    their_weights(kw_ref).wait_send()
    for m in range(1 - far, far + 1):
        _, _, to, copy = sum_send(m)
        pl.when(to != head)(copy.wait_send)
    clock[0] += 1000.0
    drain(0.0)
    for part in (0, 1):
        for i in reversed(order):
            frm = zp(i)
            region = routed_ref.at[0, frm] if part == 0 else routed_ref.at[1:, frm]
            remote(region, region, rz_s.at[part, frm], rz_r.at[part, frm], frm * NY + y, head).wait_recv()
    for copy in outs:
        copy.wait()
    fresh_out.wait()


def project(store_hidden, owner_row, new_hidden, key_columns, value_columns):
    dma = pltpu.SemaphoreType.DMA
    hbm = pl.BlockSpec(memory_space=pltpu.HBM)
    return pl.pallas_call(
        project_kernel,
        out_shape=(
            jax.ShapeDtypeStruct((NY, NZ, 2 * CAP, HD), jnp.bfloat16),
            jax.ShapeDtypeStruct((2, HD, TURN), jnp.float32),
        ),
        in_specs=[hbm] * 5,
        out_specs=(hbm, hbm),
        scratch_shapes=[
            pltpu.VMEM((ROWS, CHIP_FEAT), jnp.bfloat16),
            pltpu.VMEM((1, STORED), jnp.int32),
            pltpu.VMEM((NZ, NY, 16, CHIP_FEAT), jnp.bfloat16),
            pltpu.VMEM((NZ, NY, 16, ROWS), jnp.bfloat16),
            pltpu.VMEM((NX, 2, 2, NY, 16, ROWS), jnp.bfloat16),
            pltpu.VMEM((2 * NX, 8, ROWS), jnp.float32),
            pltpu.VMEM((HIST, STORED), jnp.bfloat16),
            pltpu.VMEM((HIST, HD), jnp.float32),
            pltpu.VMEM((2, HD, TURN), jnp.float32),
            pltpu.VMEM((NY, NZ, 2 * CAP, HD), jnp.bfloat16),
            pltpu.VMEM((NY, NZ, 2 * CAP, HD), jnp.bfloat16),
            dma((4,)), dma((5,)),
            dma((3,)), dma((3,)),
            dma((len(WAYS), NZ + 1)), dma((len(WAYS), NZ + 1)),
            dma((10, 2, 2)), dma((10, 2, 2)),
            dma((NZ,)), dma((NX, 2, 2)),
            dma((2 * NX,)), dma((2 * NX,)),
            dma((NY,)), dma((NY,)),
            dma((2, NZ)), dma((2, NZ)),
        ],
        compiler_params=pltpu.CompilerParams(
            collective_id=0, has_side_effects=True, vmem_limit_bytes=64 * 1024 * 1024
        ),
        name="project_rows",
    )(store_hidden, owner_row, new_hidden, key_columns, value_columns)


def attend_kernel(
    turn_ref, rows_ref, fresh_ref, query_ref, cos_ref, sin_ref, out_ref, key_ref, value_ref,
    rows_in, fresh_in, query_in, cos_in, sin_in, out, keys_out, values_out, in_s, out_s,
):
    def rotate(values, cosine, sine):
        return values * cosine + pltpu.roll(values, HD // 2, 1) * sine

    y = lax.rem(lax.axis_index("seq"), NY)
    fetches = [
        pltpu.make_async_copy(src, dst, in_s.at[i])
        for i, (src, dst) in enumerate(
            [(rows_ref.at[r], rows_in.at[:, lax.rem(y + r, NY)]) for r in range(NY)]
            + [(cos_ref, cos_in), (sin_ref, sin_in), (fresh_ref, fresh_in), (query_ref, query_in)]
        )
    ]
    for fetch in fetches:
        fetch.start()
    row_at = lax.broadcasted_iota(jnp.int32, (HIST, HIST), 0)
    lane_at = lax.broadcasted_iota(jnp.int32, (HIST, HIST), 1)
    before = jnp.where(lane_at < row_at, 1.0, 0.0).astype(jnp.bfloat16)
    for fetch in fetches[:NY]:
        fetch.wait()
    rows = rows_in[...].reshape(SESS, 2 * CAP, HD).astype(jnp.float32)
    sent_keys = rows[:, :CAP].reshape(HIST, HD)
    sent_values = rows[:, CAP:].reshape(HIST, HD)
    valid = jnp.abs(sent_keys) < EMPTY_TEST
    sent_keys = jnp.where(valid, sent_keys, 0.0).astype(jnp.bfloat16)
    marks = jnp.where(valid, 1.0, 0.0)
    position = jnp.dot(before, marks.astype(jnp.bfloat16), preferred_element_type=jnp.float32)
    position = jnp.where(valid, position, -1.0).T[:1].astype(jnp.int32)
    place = jnp.where(row_at == position, 1.0, 0.0).astype(jnp.bfloat16)
    history = jnp.dot(
        place,
        jnp.concatenate([sent_keys, sent_values.astype(jnp.bfloat16)], axis=1),
        preferred_element_type=jnp.float32,
    )
    length = jnp.sum(marks[:, :1]).astype(jnp.int32)
    turn = turn_ref[0]
    for fetch in fetches[NY:]:
        fetch.wait()

    keys_out[0, :HIST] = rotate(history[:, :HD], cos_in[:HIST], sin_in[:HIST]).astype(jnp.bfloat16)
    values_out[0, :HIST] = history[:, HD:].astype(jnp.bfloat16)
    cosine = cos_in[pl.ds(length, TURN), :]
    sine = sin_in[pl.ds(length, TURN), :]
    live = lax.broadcasted_iota(jnp.int32, (TURN, HD), 0) < turn
    keys_out[0, HIST:] = jnp.where(live, rotate(fresh_in[0].T, cosine, sine), 0.0).astype(jnp.bfloat16)
    values_out[0, HIST:] = jnp.where(live, fresh_in[1].T, 0.0).astype(jnp.bfloat16)
    stores = [
        pltpu.make_async_copy(keys_out, key_ref, out_s.at[0]),
        pltpu.make_async_copy(values_out, value_ref, out_s.at[1]),
    ]
    for copy in stores:
        copy.start()

    keys = keys_out[0]
    values = values_out[0]
    slot_at = lax.broadcasted_iota(jnp.int32, (TURN, CACHE), 0)
    cache_at = lax.broadcasted_iota(jnp.int32, (TURN, CACHE), 1)
    allowed = (cache_at < length) | ((cache_at >= HIST) & (cache_at - HIST <= slot_at))
    for group in range(QH // KVH):
        at = pl.ds(group * HD, HD)
        query = rotate(query_in[:, at].astype(jnp.float32), cosine, sine).astype(jnp.bfloat16)
        scores = jnp.where(allowed, nt_dot(query, keys), -jnp.inf)
        highest = jnp.max(scores, axis=1, keepdims=True)
        exponent = jnp.exp2((scores - highest) * (math.log2(math.e) / math.sqrt(HD)))
        total = jnp.sum(exponent, axis=1, keepdims=True)
        result = jnp.dot(exponent.astype(jnp.bfloat16), values, preferred_element_type=jnp.float32)
        result = result * (1.0 / total)
        out[group] = jnp.where(live, result, 0.0).astype(jnp.bfloat16)
        stores.append(pltpu.make_async_copy(out.at[group], out_ref.at[:, at], out_s.at[2 + group]))
        stores[-1].start()
    for copy in stores:
        copy.wait()


def attend(turn_length, rows, fresh, queries):
    cosine, sine = rotation_tables()
    hbm = pl.BlockSpec(memory_space=pltpu.HBM)
    groups = QH // KVH
    return pl.pallas_call(
        attend_kernel,
        out_shape=(
            jax.ShapeDtypeStruct((TURN, groups * HD), jnp.bfloat16),
            jax.ShapeDtypeStruct((1, CACHE, HD), jnp.bfloat16),
            jax.ShapeDtypeStruct((1, CACHE, HD), jnp.bfloat16),
        ),
        in_specs=[pl.BlockSpec(memory_space=pltpu.SMEM)] + [hbm] * 5,
        out_specs=(hbm, hbm, hbm),
        scratch_shapes=[
            pltpu.VMEM((NZ, NY, 2 * CAP, HD), jnp.bfloat16),
            pltpu.VMEM((2, HD, TURN), jnp.float32),
            pltpu.VMEM((TURN, groups * HD), jnp.bfloat16),
            pltpu.VMEM((CACHE, HD), jnp.float32),
            pltpu.VMEM((CACHE, HD), jnp.float32),
            pltpu.VMEM((groups, TURN, HD), jnp.bfloat16),
            pltpu.VMEM((1, CACHE, HD), jnp.bfloat16),
            pltpu.VMEM((1, CACHE, HD), jnp.bfloat16),
            pltpu.SemaphoreType.DMA((4 + NY,)),
            pltpu.SemaphoreType.DMA((2 + groups,)),
        ],
        compiler_params=pltpu.CompilerParams(vmem_limit_bytes=64 * 1024 * 1024),
        name="attend_turn",
    )(turn_length, rows, fresh, queries, jnp.asarray(cosine), jnp.asarray(sine))


def local(store_hidden, owner_map, new_hidden, new_lengths, queries, key_weight, value_weight):
    rows, fresh = project(
        store_hidden, owner_map.reshape(1, STORED), new_hidden, key_weight.T, value_weight.T
    )
    return attend(new_lengths, rows, fresh, queries)


def solution(mesh):
    placed = (
        P("seq", "head"),
        P("seq", None),
        P("seq", "head"),
        P("seq"),
        P("seq", "head"),
        P("head", "seq"),
        P("head", "seq"),
    )
    return jax.shard_map(
        local,
        mesh=mesh,
        in_specs=placed,
        out_specs=(P("seq", "head"), P("seq", None, "head"), P("seq", None, "head")),
        check_vma=False,
    )
```
